32 devices in a mesh: groups: 2 (over x), chol: 16 (over z, y, core).
Axes of the slice: x: 2, y: 2, z: 4, core: 2. Of those that a mesh axis runs over, the one named last changes fastest.
Arguments:
- green: bfloat16 [8, 256, 1024], P('groups', 'chol'), parts along dimension 0, may hold values from -6 to 6
- chol_vecs: bfloat16 [192, 256, 1024], P('chol'), may hold values from -0.15625 to 0.15625, as said below
- cotangent: float32 [8], P('groups'), parts along dimension 0, may hold values from 1536 to 6144
Outputs:
- energy: float32 [8], P('groups'), parts along dimension 0
- grad_green: float32 [8, 256, 1024], P('groups', 'chol'), parts along dimension 0
The draws below stay inside these ranges and needn't reach their ends.
There are 2 independent parts, one for each index of `groups`. The reference program is written for one: setup_inputs(seed, part) draws one part's arguments, and reference() takes and returns one part's arrays. A program takes and returns all parts, laid end to end along the dimension named above; an argument that names none is the same for every part. Nothing has to cross between parts.
Inputs may be any that keep to these rules, and one draw needn't show every extreme that they name: `chol_vecs`: each vector's entries are of order 1024 ** -0.5 times a factor that changes slowly from vector to vector.
All inputs are finite; a program needn't handle non-finite values.
Results may differ from the reference program's by a relative error of at most 0.0029.
Values may be sent and summed in bfloat16 or wider, within the bound.
A program may use at most 64 MiB of HBM per device.

```python
import math
import jax
import jax.numpy as jnp
from jax import lax

NBASIS = 1024
NOCC = 256
WALKERS = 4
NCHOL = 192


def draw_chol_vecs(key, part):
    position = jnp.arange(NCHOL, dtype=jnp.float32) / NCHOL
    values = jnp.clip(jax.random.normal(key, (NCHOL, NOCC, NBASIS), jnp.float32), -5.0, 5.0)
    decay = 3.0
    factors = decay ** (-0.5 * position)
    return (values * factors[:, None, None] * NBASIS ** (-0.5)).astype(jnp.bfloat16)


def level_of(stream_key, dims, split, smallest, largest):
    loudness, own = 1.0, jax.random.fold_in(stream_key, 6)
    for dim, shards_of in split:
        draws = jnp.exp(jax.random.uniform(jax.random.fold_in(own, dim), (shards_of,), jnp.float32, smallest / len(split), largest / len(split)))
        loudness = loudness * jnp.repeat(draws, dims[dim] // shards_of).reshape([-1 if axis == dim else 1 for axis in range(len(dims))])
    return loudness


def normal_values(rng, dims, spread, bound, shards=(), kind=jnp.bfloat16):
    result = jax.random.normal(rng, dims, jnp.float32) * spread
    if len(shards) > 0:
        result = level_of(rng, dims, shards, -0.22, 0.18) * result
    return jnp.clip(result, min=-bound, max=bound).astype(kind)


def setup_inputs(seed: int = 0, part: int = 0) -> dict:
    arg_keys = jax.random.split(jax.random.key(seed), 4)
    own_keys = jax.random.split(jax.random.fold_in(arg_keys[3], part), 4)
    return {
        "green": normal_values(own_keys[0], (WALKERS, NOCC, NBASIS), 1.0, 6.0, ((1, 16),)),
        "chol_vecs": draw_chol_vecs(jax.random.fold_in(arg_keys[3], 71), part),
        "cotangent": jnp.clip(jnp.exp(jax.random.uniform(own_keys[2], (WALKERS,), jnp.float32, math.log(1536.0), math.log(6144.0))), 1536.0, 6144.0),
    }


def reference(green, chol_vecs, cotangent):
    scale = 1.0 / (NOCC * NCHOL)
    per_block = 4 if NCHOL % 4 == 0 else 1
    blocks = chol_vecs.reshape(NCHOL // per_block, per_block, NOCC, NBASIS)
    green_wide = green.astype(jnp.float32)

    def step(carry, lblock):
        energy_acc, grad_acc = carry
        lwide = lblock.astype(jnp.float32)
        tmat = jnp.einsum('gip,wjp->wgij', lwide, green_wide)
        pairs = jnp.einsum('wgij,wgji->w', tmat, tmat)
        thalf = lax.optimization_barrier(tmat.astype(jnp.bfloat16)).astype(jnp.float32)
        gpart = jnp.einsum('wgki,gip->wkp', thalf, lwide)
        return (energy_acc + pairs, grad_acc + gpart), None

    start = (jnp.zeros((WALKERS,), jnp.float32), jnp.zeros((WALKERS, NOCC, NBASIS), jnp.float32))
    (energy_sum, grad_sum), unused = lax.scan(step, start, blocks)
    energy = -0.5 * scale * energy_sum
    grad_green = -scale * cotangent[:, None, None] * grad_sum
    return (energy, grad_green)
```

```python
import functools

import jax
import jax.numpy as jnp
from jax import lax
from jax.experimental import pallas as pl
from jax.experimental.pallas import tpu as pltpu
from jax.sharding import PartitionSpec as P

CORES = 2
COLUMNS = 2


def exchange_kernel(
    scale,
    cot_ref, green_ref, chol_ref,
    energy_ref, grad_ref,
    vecs, full, half, partial, pair, ysend, yrecv, kept, zsend, zrecv, final,
    eparts, eyparts, ezparts, erecv_c, erecv_y, erecv_z,
    load_sem, gz_send, gz_recv, gy_send, gy_recv, gc_send, gc_recv,
    rc_send, rc_recv, ry_send, ry_recv, rz_send, rz_recv,
    ec_sem, ey_sem, ez_send, ez_recv,
):
    walkers, rows, basis = green_ref.shape
    count, occupied, _ = chol_ref.shape
    planes = full.shape[1]
    bf16, f32 = jnp.bfloat16, jnp.float32

    me = lax.axis_index("chol")
    c = lax.rem(me, CORES)
    y = lax.rem(me // CORES, COLUMNS)
    z = me // (CORES * COLUMNS)

    def device(zz, yy, cc):
        return {"chol": (zz * COLUMNS + yy) * CORES + cc}

    plane = [lax.rem(z + k, planes) for k in range(planes)]
    source = [lax.rem(z - k + planes, planes) for k in range(planes)]
    over_z = [device(plane[k], y, c) for k in range(1, planes)]
    over_y = device(z, 1 - y, c)
    over_c = device(z, y, 1 - c)

    loads = load_sem.shape[0]
    per = count // loads
    for i in range(loads):
        pltpu.make_async_copy(
            chol_ref.at[pl.ds(i * per, per)], vecs.at[pl.ds(i * per, per)], load_sem.at[i]
        ).start()
    for w in range(walkers):
        full[w, z, y, c] = green_ref[w]

    barrier = pltpu.get_barrier_semaphore()
    for peer in over_z + [over_y, over_c]:
        pl.semaphore_signal(barrier, inc=1, device_id=peer, device_id_type=pl.DeviceIdType.MESH)
    pl.semaphore_wait(barrier, planes + 1)

    sent = []

    def send(src, dst, send_sem, recv_sem, peer):
        copy = pltpu.make_async_remote_copy(
            src_ref=src, dst_ref=dst, send_sem=send_sem, recv_sem=recv_sem,
            device_id=peer, device_id_type=pl.DeviceIdType.MESH,
        )
        copy.start()
        sent.append(copy)
        return copy

    gz = [[None] * planes for _ in range(walkers)]
    gy = [[None] * planes for _ in range(walkers)]
    gc = [[None] * COLUMNS for _ in range(walkers)]

    def pass_y(w, k):
        block = full.at[w, source[k], y, c]
        gy[w][k] = send(block, block, gy_send.at[w, k], gy_recv.at[w, k], over_y)

    for w in range(walkers):
        block = full.at[w, z, y, c]
        for k in range(planes - 1, 0, -1):
            gz[w][k] = send(block, block, gz_send.at[w, k - 1], gz_recv.at[w, k - 1], over_z[k - 1])
        pass_y(w, 0)

    def gather_z(w):
        for k in range(1, planes):
            gz[w][k].wait_recv()
            pass_y(w, k)
        own = full.at[w, :, y, c]
        gc[w][0] = send(own, own, gc_send.at[w, 0], gc_recv.at[w, 0], over_c)

    def gather_y(w):
        for k in range(planes):
            gy[w][k].wait_recv()
        other = full.at[w, :, 1 - y, c]
        gc[w][1] = send(other, other, gc_send.at[w, 1], gc_recv.at[w, 1], over_c)

    def gather_c(w):
        for k in range(COLUMNS):
            gc[w][k].wait_recv()

    def make_tmat(w):
        eparts[w] = jnp.zeros_like(eparts[w])

        @pl.loop(0, loads)
        def _(i):
            first = i * per
            if w == 0:
                pltpu.make_async_copy(
                    chol_ref.at[pl.ds(first, per)], vecs.at[pl.ds(first, per)], load_sem.at[i]
                ).wait()
            left = vecs[pl.ds(first, per)].reshape(per * occupied, basis)
            right = full[w].reshape(occupied, basis)
            tmat = lax.dot_general(left, right, (((1,), (1,)), ((), ())), preferred_element_type=f32)
            total = jnp.zeros(eparts.shape[1:], f32)
            for j in range(per):
                one = tmat[j * occupied:(j + 1) * occupied]
                at = pl.multiple_of((first + j) * occupied, occupied)
                half[:, pl.ds(at, occupied)] = one.astype(bf16)
                pairs = one * one.T
                folded = pairs.reshape(occupied // 8, 8, occupied).sum(axis=0)
                for lane in range(0, occupied, 128):
                    total += folded[:, lane:lane + 128]
            eparts[w] += total

    chunk = 256 if basis % 256 == 0 else 128

    def make_grad(w):
        @pl.loop(0, basis // chunk)
        def _(i):
            at = pl.multiple_of(i * chunk, chunk)
            right = vecs[:, :, pl.ds(at, chunk)].reshape(count * occupied, chunk)
            part = jnp.dot(half[...], right, preferred_element_type=f32)
            for zz in range(planes):
                for yy in range(COLUMNS):
                    for cc in range(CORES):
                        row = ((zz * COLUMNS + yy) * CORES + cc) * rows
                        partial[w, cc, yy, zz, :, pl.ds(at, chunk)] = part[row:row + rows]

    rc, ry = [None] * walkers, [None] * walkers
    rz = [[None] * planes for _ in range(walkers)]

    def reduce_c(w):
        rc[w] = send(partial.at[w, 1 - c], pair.at[w], rc_send.at[w], rc_recv.at[w], over_c)

    def reduce_y(w):
        rc[w].wait_recv()
        ysend[w] = (partial[w, c, 1 - y] + pair[w, 1 - y]).astype(bf16)
        ry[w] = send(ysend.at[w], yrecv.at[w], ry_send.at[w], ry_recv.at[w], over_y)
        kept[w] = partial[w, c, y] + pair[w, y]

    def reduce_z(w):
        ry[w].wait_recv()
        zsend[w] = (kept[w] + yrecv[w].astype(f32)).astype(bf16)
        for k in range(planes - 1, 0, -1):
            rz[w][k] = send(
                zsend.at[w, plane[k]], zrecv.at[w, k - 1], rz_send.at[w, k - 1], rz_recv.at[w, k - 1], over_z[k - 1]
            )
        final[w] = kept[w, z] + yrecv[w, z].astype(f32)

    def finish(w):
        total = final[w]
        for k in range(1, planes):
            rz[w][k].wait_recv()
            total += zrecv[w, k - 1].astype(f32)
        grad_ref[w] = (-scale * cot_ref[w]) * total

    last = walkers - 1
    gather_z(0)
    if walkers > 1:
        gather_z(1)
    gather_y(0)
    gather_c(0)
    for w in range(walkers):
        make_tmat(w)
        if w > 0:
            reduce_y(w - 1)
        if w > 1:
            finish(w - 2)
        if w == last:
            ec = send(eparts, erecv_c, ec_sem.at[0], ec_sem.at[1], over_c)
        if w + 2 < walkers:
            gather_z(w + 2)
        if w + 1 < walkers:
            gather_y(w + 1)
        make_grad(w)
        reduce_c(w)
        if w > 0:
            reduce_z(w - 1)
        if w + 1 < walkers:
            gather_c(w + 1)
    ec.wait_recv()
    eyparts[...] = eparts[...] + erecv_c[...]
    ey = send(eyparts, erecv_y, ey_sem.at[0], ey_sem.at[1], over_y)
    reduce_y(last)
    if last > 0:
        finish(last - 1)
    ey.wait_recv()
    ezparts[...] = eyparts[...] + erecv_y[...]
    ez = [
        send(ezparts, erecv_z.at[k - 1], ez_send.at[k - 1], ez_recv.at[k - 1], over_z[k - 1])
        for k in range(1, planes)
    ]
    reduce_z(last)
    esum = ezparts[...]
    for k in range(1, planes):
        ez[k - 1].wait_recv()
        esum += erecv_z[k - 1]
    for w in range(walkers):
        energy_ref[w] = -0.5 * scale * jnp.sum(esum[w])
    finish(last)
    for copy in sent:
        copy.wait_send()


def per_device_kernel(green, chol_vecs, cotangent):
    walkers, rows, basis = green.shape
    count, occupied, _ = chol_vecs.shape
    devices = lax.axis_size("chol")
    planes = devices // (CORES * COLUMNS)
    scale = 1.0 / (occupied * count * devices)
    per = max(i for i in (1, 2, 3) if count % i == 0)
    loads = count // per
    bf16, f32 = jnp.bfloat16, jnp.float32
    block = (rows, basis)
    dma = pltpu.SemaphoreType.DMA
    others = planes - 1
    estack = (walkers, 8, 128)
    energy, grad_green = pl.pallas_call(
        functools.partial(exchange_kernel, scale),
        out_shape=(
            jax.ShapeDtypeStruct((walkers,), f32),
            jax.ShapeDtypeStruct((walkers,) + block, f32),
        ),
        in_specs=[
            pl.BlockSpec(memory_space=pltpu.SMEM),
            pl.BlockSpec(memory_space=pltpu.VMEM),
            pl.BlockSpec(memory_space=pl.ANY),
        ],
        out_specs=(
            pl.BlockSpec(memory_space=pltpu.SMEM),
            pl.BlockSpec(memory_space=pltpu.VMEM),
        ),
        scratch_shapes=[
            pltpu.VMEM((count, occupied, basis), bf16),
            pltpu.VMEM((walkers, planes, COLUMNS, CORES) + block, bf16),
            pltpu.VMEM((occupied, count * occupied), bf16),
            pltpu.VMEM((walkers, CORES, COLUMNS, planes) + block, f32),
            pltpu.VMEM((walkers, COLUMNS, planes) + block, f32),
            pltpu.VMEM((walkers, planes) + block, bf16),
            pltpu.VMEM((walkers, planes) + block, bf16),
            pltpu.VMEM((walkers, planes) + block, f32),
            pltpu.VMEM((walkers, planes) + block, bf16),
            pltpu.VMEM((walkers, others) + block, bf16),
            pltpu.VMEM((walkers,) + block, f32),
            pltpu.VMEM(estack, f32),
            pltpu.VMEM(estack, f32),
            pltpu.VMEM(estack, f32),
            pltpu.VMEM(estack, f32),
            pltpu.VMEM(estack, f32),
            pltpu.VMEM((others,) + estack, f32),
            dma((loads,)),
            dma((walkers, others)), dma((walkers, others)),
            dma((walkers, planes)), dma((walkers, planes)),
            dma((walkers, COLUMNS)), dma((walkers, COLUMNS)),
            dma((walkers,)), dma((walkers,)),
            dma((walkers,)), dma((walkers,)),
            dma((walkers, others)), dma((walkers, others)),
            dma((2,)), dma((2,)),
            dma((others,)), dma((others,)),
        ],
        compiler_params=pltpu.CompilerParams(
            collective_id=0, has_side_effects=True, vmem_limit_bytes=48 * 1024 * 1024
        ),
        cost_estimate=pl.CostEstimate(
            flops=4 * walkers * count * occupied * occupied * basis,
            bytes_accessed=2 * chol_vecs.size,
            transcendentals=0,
        ),
    )(cotangent, green, chol_vecs)
    return (energy, grad_green)


def per_device_plain(green, chol_vecs, cotangent):
    count = chol_vecs.shape[0]
    walkers = green.shape[0]
    occupied = chol_vecs.shape[1]
    basis = chol_vecs.shape[2]
    scale = 1.0 / (occupied * count * lax.axis_size("chol"))
    full_green = lax.all_gather(green, "chol", axis=1, tiled=True)
    per_block = 4 if count % 4 == 0 else 1
    blocks = chol_vecs.reshape(count // per_block, per_block, occupied, basis)

    def step(carry, lblock):
        energy_acc, grad_acc = carry
        tmat = jnp.einsum("gip,wjp->wgij", lblock, full_green, preferred_element_type=jnp.float32)
        pairs = jnp.einsum("wgij,wgji->w", tmat, tmat)
        thalf = tmat.astype(jnp.bfloat16)
        gpart = jnp.einsum("wgki,gip->wkp", thalf, lblock, preferred_element_type=jnp.float32)
        return ((energy_acc + pairs, grad_acc + gpart), None)

    start = (jnp.zeros((walkers,), jnp.float32), jnp.zeros((walkers, occupied, basis), jnp.float32))
    (energy_part, grad_part), unused = lax.scan(step, start, blocks)
    energy_sum = lax.psum(energy_part, "chol")
    own_rows = lax.psum_scatter(grad_part, "chol", scatter_dimension=1, tiled=True)
    energy = -0.5 * scale * energy_sum
    grad_green = -scale * cotangent[:, None, None] * own_rows
    return (energy, grad_green)


def per_device(green, chol_vecs, cotangent):
    devices = lax.axis_size("chol")
    fits = (
        devices % (CORES * COLUMNS) == 0
        and devices > CORES * COLUMNS
        and green.shape[1] % 16 == 0
        and chol_vecs.shape[1] % 128 == 0
        and chol_vecs.shape[2] % 128 == 0
    )
    run = per_device_kernel if fits else per_device_plain
    return run(green, chol_vecs, cotangent)


def solution(mesh):
    placed = (P("groups", "chol", None), P("chol", None, None), P("groups"))
    return jax.shard_map(
        per_device,
        mesh=mesh,
        in_specs=placed,
        out_specs=(P("groups"), P("groups", "chol", None)),
        check_vma=False,
    )
```

```python
import functools

import jax
import jax.numpy as jnp
from jax import lax
from jax.experimental import pallas as pl
from jax.experimental.pallas import tpu as pltpu
from jax.sharding import PartitionSpec as P

CORES = 2
COLUMNS = 2


def exchange_kernel(
    scale,
    green_ref, chol_ref,
    energy_ref, grad_ref,
    vecs, full, half, partial, pair, ysend, yrecv, kept, zsend, zrecv, final,
    eparts, eyparts, ezparts, erecv_c, erecv_y, erecv_z,
    load_sem, own_sem, gz_send, gz_recv, gy_send, gy_recv, gc_send, gc_recv,
    rc_send, rc_recv, ry_send, ry_recv, rz_send, rz_recv,
    ec_sem, ey_sem, ez_send, ez_recv,
):
    walkers, rows, basis = green_ref.shape
    count, occupied, _ = chol_ref.shape
    planes = full.shape[1]
    bf16, f32 = jnp.bfloat16, jnp.float32

    me = lax.axis_index("chol")
    c = lax.rem(me, CORES)
    y = lax.rem(me // CORES, COLUMNS)
    z = me // (CORES * COLUMNS)

    def device(zz, yy, cc):
        return {"chol": (zz * COLUMNS + yy) * CORES + cc}

    plane = [lax.rem(z + k, planes) for k in range(planes)]
    source = [lax.rem(z - k + planes, planes) for k in range(planes)]
    over_z = [device(plane[k], y, c) for k in range(1, planes)]
    over_y = device(z, 1 - y, c)
    over_c = device(z, y, 1 - c)

    own = [pltpu.make_async_copy(green_ref.at[w], full.at[w, z, y, c], own_sem.at[w]) for w in range(walkers)]
    for copy in own:
        copy.start()
    loads = load_sem.shape[0]
    per = count // loads
    for i in range(loads):
        pltpu.make_async_copy(
            chol_ref.at[pl.ds(i * per, per)], vecs.at[pl.ds(i * per, per)], load_sem.at[i]
        ).start()

    barrier = pltpu.get_barrier_semaphore()
    for peer in over_z + [over_y, over_c]:
        pl.semaphore_signal(barrier, inc=1, device_id=peer, device_id_type=pl.DeviceIdType.MESH)
    pl.semaphore_wait(barrier, planes + 1)

    sent = []

    def send(src, dst, send_sem, recv_sem, peer):
        copy = pltpu.make_async_remote_copy(
            src_ref=src, dst_ref=dst, send_sem=send_sem, recv_sem=recv_sem,
            device_id=peer, device_id_type=pl.DeviceIdType.MESH,
        )
        copy.start()
        sent.append(copy)
        return copy

    gz = [[None] * planes for _ in range(walkers)]
    gy = [[None] * planes for _ in range(walkers)]
    gc = [[None] * COLUMNS for _ in range(walkers)]

    def pass_y(w, k):
        block = full.at[w, source[k], y, c]
        gy[w][k] = send(block, block, gy_send.at[w, k], gy_recv.at[w, k], over_y)

    for w in range(walkers):
        own[w].wait()
        block = full.at[w, z, y, c]
        for k in range(planes - 1, 0, -1):
            gz[w][k] = send(block, block, gz_send.at[w, k - 1], gz_recv.at[w, k - 1], over_z[k - 1])
        pass_y(w, 0)

    def gather_z(w):
        for k in range(1, planes):
            gz[w][k].wait_recv()
            pass_y(w, k)
        own = full.at[w, :, y, c]
        gc[w][0] = send(own, own, gc_send.at[w, 0], gc_recv.at[w, 0], over_c)

    def gather_y(w):
        for k in range(planes):
            gy[w][k].wait_recv()
        other = full.at[w, :, 1 - y, c]
        gc[w][1] = send(other, other, gc_send.at[w, 1], gc_recv.at[w, 1], over_c)

    def gather_c(w):
        for k in range(COLUMNS):
            gc[w][k].wait_recv()

    def make_tmat(w):
        @pl.loop(0, loads)
        def _(i):
            first = i * per
            if w == 0:
                pltpu.make_async_copy(
                    chol_ref.at[pl.ds(first, per)], vecs.at[pl.ds(first, per)], load_sem.at[i]
                ).wait()
            left = vecs[pl.ds(first, per)].reshape(per * occupied, basis)
            right = full[w].reshape(occupied, basis)
            tmat = lax.dot_general(left, right, (((1,), (1,)), ((), ())), preferred_element_type=f32)
            for j in range(per):
                one = tmat[j * occupied:(j + 1) * occupied]
                at = pl.multiple_of((first + j) * occupied, occupied)
                half[:, pl.ds(at, occupied)] = one.astype(bf16)

    chunk = 256 if basis % 256 == 0 else 128

    def make_grad(w):
        eparts[w] = jnp.zeros_like(eparts[w])

        @pl.loop(0, basis // chunk)
        def _(i):
            at = pl.multiple_of(i * chunk, chunk)
            right = vecs[:, :, pl.ds(at, chunk)].reshape(count * occupied, chunk)
            part = jnp.dot(half[...], right, preferred_element_type=f32)
            green = full[w, :, :, :, :, pl.ds(at, chunk)].reshape(occupied, chunk)
            folded = (part * green.astype(f32)).reshape(occupied // 8, 8, chunk).sum(axis=0)
            for lane in range(0, chunk, 128):
                eparts[w] += folded[:, lane:lane + 128]
            for zz in range(planes):
                for yy in range(COLUMNS):
                    for cc in range(CORES):
                        row = ((zz * COLUMNS + yy) * CORES + cc) * rows
                        partial[w, cc, yy, zz, :, pl.ds(at, chunk)] = part[row:row + rows]

    rc, ry = [None] * walkers, [None] * walkers
    rz = [[None] * planes for _ in range(walkers)]

    def reduce_c(w):
        rc[w] = send(partial.at[w, 1 - c], pair.at[w], rc_send.at[w], rc_recv.at[w], over_c)

    def reduce_y(w):
        rc[w].wait_recv()
        ysend[w] = (partial[w, c, 1 - y] + pair[w, 1 - y]).astype(bf16)
        ry[w] = send(ysend.at[w], yrecv.at[w], ry_send.at[w], ry_recv.at[w], over_y)
        kept[w] = partial[w, c, y] + pair[w, y]

    def reduce_z(w):
        ry[w].wait_recv()
        zsend[w] = (kept[w] + yrecv[w].astype(f32)).astype(bf16)
        for k in range(planes - 1, 0, -1):
            rz[w][k] = send(
                zsend.at[w, plane[k]], zrecv.at[w, k - 1], rz_send.at[w, k - 1], rz_recv.at[w, k - 1], over_z[k - 1]
            )
        final[w] = kept[w, z] + yrecv[w, z].astype(f32)

    def finish(w):
        total = final[w]
        for k in range(1, planes):
            rz[w][k].wait_recv()
            total += zrecv[w, k - 1].astype(f32)
        grad_ref[w] = -scale * total

    last = walkers - 1
    gather_z(0)
    if walkers > 1:
        gather_z(1)
    gather_y(0)
    gather_c(0)
    for w in range(walkers):
        make_tmat(w)
        if w > 0:
            reduce_y(w - 1)
        if w > 1:
            finish(w - 2)
        if w + 2 < walkers:
            gather_z(w + 2)
        if w + 1 < walkers:
            gather_y(w + 1)
        make_grad(w)
        if w == last:
            ec = send(eparts, erecv_c, ec_sem.at[0], ec_sem.at[1], over_c)
        reduce_c(w)
        if w > 0:
            reduce_z(w - 1)
        if w + 1 < walkers:
            gather_c(w + 1)
    ec.wait_recv()
    eyparts[...] = eparts[...] + erecv_c[...]
    ey = send(eyparts, erecv_y, ey_sem.at[0], ey_sem.at[1], over_y)
    reduce_y(last)
    if last > 0:
        finish(last - 1)
    ey.wait_recv()
    ezparts[...] = eyparts[...] + erecv_y[...]
    ez = [
        send(ezparts, erecv_z.at[k - 1], ez_send.at[k - 1], ez_recv.at[k - 1], over_z[k - 1])
        for k in range(1, planes)
    ]
    reduce_z(last)
    esum = ezparts[...]
    for k in range(1, planes):
        ez[k - 1].wait_recv()
        esum += erecv_z[k - 1]
    energy_ref[...] = -0.5 * scale * esum
    finish(last)
    for copy in sent:
        copy.wait_send()


def per_device_kernel(green, chol_vecs, cotangent):
    walkers, rows, basis = green.shape
    count, occupied, _ = chol_vecs.shape
    devices = lax.axis_size("chol")
    planes = devices // (CORES * COLUMNS)
    scale = 1.0 / (occupied * count * devices)
    per = max(i for i in (1, 2, 3) if count % i == 0)
    loads = count // per
    bf16, f32 = jnp.bfloat16, jnp.float32
    block = (rows, basis)
    dma = pltpu.SemaphoreType.DMA
    others = planes - 1
    estack = (walkers, 8, 128)
    energy_parts, own_rows = pl.pallas_call(
        functools.partial(exchange_kernel, scale),
        out_shape=(
            jax.ShapeDtypeStruct(estack, f32),
            jax.ShapeDtypeStruct((walkers,) + block, f32),
        ),
        in_specs=[
            pl.BlockSpec(memory_space=pl.ANY),
            pl.BlockSpec(memory_space=pl.ANY),
        ],
        out_specs=(
            pl.BlockSpec(memory_space=pltpu.VMEM),
            pl.BlockSpec(memory_space=pltpu.VMEM),
        ),
        scratch_shapes=[
            pltpu.VMEM((count, occupied, basis), bf16),
            pltpu.VMEM((walkers, planes, COLUMNS, CORES) + block, bf16),
            pltpu.VMEM((occupied, count * occupied), bf16),
            pltpu.VMEM((walkers, CORES, COLUMNS, planes) + block, f32),
            pltpu.VMEM((walkers, COLUMNS, planes) + block, f32),
            pltpu.VMEM((walkers, planes) + block, bf16),
            pltpu.VMEM((walkers, planes) + block, bf16),
            pltpu.VMEM((walkers, planes) + block, f32),
            pltpu.VMEM((walkers, planes) + block, bf16),
            pltpu.VMEM((walkers, others) + block, bf16),
            pltpu.VMEM((walkers,) + block, f32),
            pltpu.VMEM(estack, f32),
            pltpu.VMEM(estack, f32),
            pltpu.VMEM(estack, f32),
            pltpu.VMEM(estack, f32),
            pltpu.VMEM(estack, f32),
            pltpu.VMEM((others,) + estack, f32),
            dma((loads,)), dma((walkers,)),
            dma((walkers, others)), dma((walkers, others)),
            dma((walkers, planes)), dma((walkers, planes)),
            dma((walkers, COLUMNS)), dma((walkers, COLUMNS)),
            dma((walkers,)), dma((walkers,)),
            dma((walkers,)), dma((walkers,)),
            dma((walkers, others)), dma((walkers, others)),
            dma((2,)), dma((2,)),
            dma((others,)), dma((others,)),
        ],
        compiler_params=pltpu.CompilerParams(
            collective_id=0, has_side_effects=True, vmem_limit_bytes=60 * 1024 * 1024
        ),
        cost_estimate=pl.CostEstimate(
            flops=4 * walkers * count * occupied * occupied * basis,
            bytes_accessed=2 * chol_vecs.size,
            transcendentals=0,
        ),
    )(green, chol_vecs)
    energy = jnp.sum(energy_parts, axis=(1, 2))
    grad_green = cotangent[:, None, None] * own_rows
    return (energy, grad_green)


def per_device_plain(green, chol_vecs, cotangent):
    count = chol_vecs.shape[0]
    walkers = green.shape[0]
    occupied = chol_vecs.shape[1]
    basis = chol_vecs.shape[2]
    scale = 1.0 / (occupied * count * lax.axis_size("chol"))
    full_green = lax.all_gather(green, "chol", axis=1, tiled=True)
    per_block = 4 if count % 4 == 0 else 1
    blocks = chol_vecs.reshape(count // per_block, per_block, occupied, basis)

    def step(carry, lblock):
        energy_acc, grad_acc = carry
        tmat = jnp.einsum("gip,wjp->wgij", lblock, full_green, preferred_element_type=jnp.float32)
        pairs = jnp.einsum("wgij,wgji->w", tmat, tmat)
        thalf = tmat.astype(jnp.bfloat16)
        gpart = jnp.einsum("wgki,gip->wkp", thalf, lblock, preferred_element_type=jnp.float32)
        return ((energy_acc + pairs, grad_acc + gpart), None)

    start = (jnp.zeros((walkers,), jnp.float32), jnp.zeros((walkers, occupied, basis), jnp.float32))
    (energy_part, grad_part), unused = lax.scan(step, start, blocks)
    energy_sum = lax.psum(energy_part, "chol")
    own_rows = lax.psum_scatter(grad_part, "chol", scatter_dimension=1, tiled=True)
    energy = -0.5 * scale * energy_sum
    grad_green = -scale * cotangent[:, None, None] * own_rows
    return (energy, grad_green)


def per_device(green, chol_vecs, cotangent):
    devices = lax.axis_size("chol")
    fits = (
        devices % (CORES * COLUMNS) == 0
        and devices > CORES * COLUMNS
        and green.shape[1] % 16 == 0
        and chol_vecs.shape[1] % 128 == 0
        and chol_vecs.shape[2] % 128 == 0
    )
    run = per_device_kernel if fits else per_device_plain
    return run(green, chol_vecs, cotangent)


def solution(mesh):
    placed = (P("groups", "chol", None), P("chol", None, None), P("groups"))
    return jax.shard_map(
        per_device,
        mesh=mesh,
        in_specs=placed,
        out_specs=(P("groups"), P("groups", "chol", None)),
        check_vma=False,
    )
```

```python
import functools

import jax
import jax.numpy as jnp
from jax import lax
from jax.experimental import pallas as pl
from jax.experimental.pallas import tpu as pltpu
from jax.sharding import PartitionSpec as P

CORES = 2
COLUMNS = 2


def exchange_kernel(
    scale,
    green_ref, chol_ref,
    energy_ref, grad_ref,
    vecs, full, half, partial, pair, ysend, yrecv, kept, zsend, zrecv, final,
    eparts, eyparts, ezparts, erecv_c, erecv_y, erecv_z,
    load_sem, own_sem, gz_send, gz_recv, gy_send, gy_recv, gc_send, gc_recv,
    rc_send, rc_recv, ry_send, ry_recv, rz_send, rz_recv,
    ec_sem, ey_sem, ez_send, ez_recv,
):
    walkers, rows, basis = green_ref.shape
    count, occupied, _ = chol_ref.shape
    planes = full.shape[1]
    bf16, f32 = jnp.bfloat16, jnp.float32

    me = lax.axis_index("chol")
    c = lax.rem(me, CORES)
    y = lax.rem(me // CORES, COLUMNS)
    z = me // (CORES * COLUMNS)

    def device(zz, yy, cc):
        return {"chol": (zz * COLUMNS + yy) * CORES + cc}

    plane = [lax.rem(z + k, planes) for k in range(planes)]
    source = [lax.rem(z - k + planes, planes) for k in range(planes)]
    over_z = [device(plane[k], y, c) for k in range(1, planes)]
    over_y = device(z, 1 - y, c)
    over_c = device(z, y, 1 - c)

    own = [pltpu.make_async_copy(green_ref.at[w], full.at[w, z, y, c], own_sem.at[w]) for w in range(walkers)]
    for copy in own:
        copy.start()
    loads = load_sem.shape[0]
    per = count // loads
    for i in range(loads):
        pltpu.make_async_copy(
            chol_ref.at[pl.ds(i * per, per)], vecs.at[pl.ds(i * per, per)], load_sem.at[i]
        ).start()

    barrier = pltpu.get_barrier_semaphore()
    for peer in over_z + [over_y, over_c]:
        pl.semaphore_signal(barrier, inc=1, device_id=peer, device_id_type=pl.DeviceIdType.MESH)
    pl.semaphore_wait(barrier, planes + 1)

    sent = []

    def send(src, dst, send_sem, recv_sem, peer):
        copy = pltpu.make_async_remote_copy(
            src_ref=src, dst_ref=dst, send_sem=send_sem, recv_sem=recv_sem,
            device_id=peer, device_id_type=pl.DeviceIdType.MESH,
        )
        copy.start()
        sent.append(copy)
        return copy

    gz = [[None] * planes for _ in range(walkers)]
    gy = [[None] * planes for _ in range(walkers)]
    gc = [[None] * COLUMNS for _ in range(walkers)]

    def pass_y(w, k):
        block = full.at[w, source[k], y, c]
        gy[w][k] = send(block, block, gy_send.at[w, k], gy_recv.at[w, k], over_y)

    def offer(w):
        own[w].wait()
        block = full.at[w, z, y, c]
        for k in range(planes - 1, 0, -1):
            gz[w][k] = send(block, block, gz_send.at[w, k - 1], gz_recv.at[w, k - 1], over_z[k - 1])
        pass_y(w, 0)

    for w in range(min(2, walkers)):
        offer(w)

    def gather_z(w):
        for k in range(1, planes):
            gz[w][k].wait_recv()
            pass_y(w, k)
        if w + 2 < walkers:
            offer(w + 2)
        own = full.at[w, :, y, c]
        gc[w][0] = send(own, own, gc_send.at[w, 0], gc_recv.at[w, 0], over_c)

    def gather_y(w):
        for k in range(planes):
            gy[w][k].wait_recv()
        other = full.at[w, :, 1 - y, c]
        gc[w][1] = send(other, other, gc_send.at[w, 1], gc_recv.at[w, 1], over_c)

    def gather_c(w):
        for k in range(COLUMNS):
            gc[w][k].wait_recv()

    def make_tmat(w):
        @pl.loop(0, loads)
        def _(i):
            first = i * per
            if w == 0:
                pltpu.make_async_copy(
                    chol_ref.at[pl.ds(first, per)], vecs.at[pl.ds(first, per)], load_sem.at[i]
                ).wait()
            left = vecs[pl.ds(first, per)].reshape(per * occupied, basis)
            right = full[w].reshape(occupied, basis)
            tmat = lax.dot_general(left, right, (((1,), (1,)), ((), ())), preferred_element_type=f32)
            for j in range(per):
                one = tmat[j * occupied:(j + 1) * occupied]
                at = pl.multiple_of((first + j) * occupied, occupied)
                half[:, pl.ds(at, occupied)] = one.astype(bf16)

    chunk = 256 if basis % 256 == 0 else 128

    def make_grad(w):
        eparts[w] = jnp.zeros_like(eparts[w])

        @pl.loop(0, basis // chunk)
        def _(i):
            at = pl.multiple_of(i * chunk, chunk)
            right = vecs[:, :, pl.ds(at, chunk)].reshape(count * occupied, chunk)
            part = jnp.dot(half[...], right, preferred_element_type=f32)
            green = full[w, :, :, :, :, pl.ds(at, chunk)].reshape(occupied, chunk)
            folded = (part * green.astype(f32)).reshape(occupied // 8, 8, chunk).sum(axis=0)
            for lane in range(0, chunk, 128):
                eparts[w] += folded[:, lane:lane + 128]
            for zz in range(planes):
                for yy in range(COLUMNS):
                    for cc in range(CORES):
                        row = ((zz * COLUMNS + yy) * CORES + cc) * rows
                        partial[w, cc, yy, zz, :, pl.ds(at, chunk)] = part[row:row + rows]

    rc, ry = [None] * walkers, [None] * walkers
    rz = [[None] * planes for _ in range(walkers)]

    def reduce_c(w):
        rc[w] = send(partial.at[w, 1 - c], pair.at[w], rc_send.at[w], rc_recv.at[w], over_c)

    def reduce_y(w):
        rc[w].wait_recv()
        ysend[w] = (partial[w, c, 1 - y] + pair[w, 1 - y]).astype(bf16)
        ry[w] = send(ysend.at[w], yrecv.at[w], ry_send.at[w], ry_recv.at[w], over_y)
        kept[w] = partial[w, c, y] + pair[w, y]

    def reduce_z(w):
        ry[w].wait_recv()
        zsend[w] = (kept[w] + yrecv[w].astype(f32)).astype(bf16)
        for k in range(planes - 1, 0, -1):
            rz[w][k] = send(
                zsend.at[w, plane[k]], zrecv.at[w, k - 1], rz_send.at[w, k - 1], rz_recv.at[w, k - 1], over_z[k - 1]
            )
        final[w] = kept[w, z] + yrecv[w, z].astype(f32)

    def finish(w):
        total = final[w]
        for k in range(1, planes):
            rz[w][k].wait_recv()
            total += zrecv[w, k - 1].astype(f32)
        grad_ref[w] = -scale * total

    last = walkers - 1
    gather_z(0)
    if walkers > 1:
        gather_z(1)
    gather_y(0)
    gather_c(0)
    for w in range(walkers):
        make_tmat(w)
        if w > 0:
            reduce_y(w - 1)
        if w > 1:
            finish(w - 2)
        if w + 2 < walkers:
            gather_z(w + 2)
        if w + 1 < walkers:
            gather_y(w + 1)
        make_grad(w)
        if w == last:
            ec = send(eparts, erecv_c, ec_sem.at[0], ec_sem.at[1], over_c)
        reduce_c(w)
        if w > 0:
            reduce_z(w - 1)
        if w + 1 < walkers:
            gather_c(w + 1)
    ec.wait_recv()
    eyparts[...] = eparts[...] + erecv_c[...]
    ey = send(eyparts, erecv_y, ey_sem.at[0], ey_sem.at[1], over_y)
    reduce_y(last)
    if last > 0:
        finish(last - 1)
    ey.wait_recv()
    ezparts[...] = eyparts[...] + erecv_y[...]
    ez = [
        send(ezparts, erecv_z.at[k - 1], ez_send.at[k - 1], ez_recv.at[k - 1], over_z[k - 1])
        for k in range(1, planes)
    ]
    reduce_z(last)
    esum = ezparts[...]
    for k in range(1, planes):
        ez[k - 1].wait_recv()
        esum += erecv_z[k - 1]
    energy_ref[...] = -0.5 * scale * esum
    finish(last)
    for copy in sent:
        copy.wait_send()


def per_device_kernel(green, chol_vecs, cotangent):
    walkers, rows, basis = green.shape
    count, occupied, _ = chol_vecs.shape
    devices = lax.axis_size("chol")
    planes = devices // (CORES * COLUMNS)
    scale = 1.0 / (occupied * count * devices)
    per = max(i for i in (1, 2, 3) if count % i == 0)
    loads = count // per
    bf16, f32 = jnp.bfloat16, jnp.float32
    block = (rows, basis)
    dma = pltpu.SemaphoreType.DMA
    others = planes - 1
    estack = (walkers, 8, 128)
    energy_parts, own_rows = pl.pallas_call(
        functools.partial(exchange_kernel, scale),
        out_shape=(
            jax.ShapeDtypeStruct(estack, f32),
            jax.ShapeDtypeStruct((walkers,) + block, f32),
        ),
        in_specs=[
            pl.BlockSpec(memory_space=pl.ANY),
            pl.BlockSpec(memory_space=pl.ANY),
        ],
        out_specs=(
            pl.BlockSpec(memory_space=pltpu.VMEM),
            pl.BlockSpec(memory_space=pltpu.VMEM),
        ),
        scratch_shapes=[
            pltpu.VMEM((count, occupied, basis), bf16),
            pltpu.VMEM((walkers, planes, COLUMNS, CORES) + block, bf16),
            pltpu.VMEM((occupied, count * occupied), bf16),
            pltpu.VMEM((walkers, CORES, COLUMNS, planes) + block, f32),
            pltpu.VMEM((walkers, COLUMNS, planes) + block, f32),
            pltpu.VMEM((walkers, planes) + block, bf16),
            pltpu.VMEM((walkers, planes) + block, bf16),
            pltpu.VMEM((walkers, planes) + block, f32),
            pltpu.VMEM((walkers, planes) + block, bf16),
            pltpu.VMEM((walkers, others) + block, bf16),
            pltpu.VMEM((walkers,) + block, f32),
            pltpu.VMEM(estack, f32),
            pltpu.VMEM(estack, f32),
            pltpu.VMEM(estack, f32),
            pltpu.VMEM(estack, f32),
            pltpu.VMEM(estack, f32),
            pltpu.VMEM((others,) + estack, f32),
            dma((loads,)), dma((walkers,)),
            dma((walkers, others)), dma((walkers, others)),
            dma((walkers, planes)), dma((walkers, planes)),
            dma((walkers, COLUMNS)), dma((walkers, COLUMNS)),
            dma((walkers,)), dma((walkers,)),
            dma((walkers,)), dma((walkers,)),
            dma((walkers, others)), dma((walkers, others)),
            dma((2,)), dma((2,)),
            dma((others,)), dma((others,)),
        ],
        compiler_params=pltpu.CompilerParams(
            collective_id=0, has_side_effects=True, vmem_limit_bytes=60 * 1024 * 1024
        ),
        cost_estimate=pl.CostEstimate(
            flops=4 * walkers * count * occupied * occupied * basis,
            bytes_accessed=2 * chol_vecs.size,
            transcendentals=0,
        ),
    )(green, chol_vecs)
    energy = jnp.sum(energy_parts, axis=(1, 2))
    grad_green = cotangent[:, None, None] * own_rows
    return (energy, grad_green)


def per_device_plain(green, chol_vecs, cotangent):
    count = chol_vecs.shape[0]
    walkers = green.shape[0]
    occupied = chol_vecs.shape[1]
    basis = chol_vecs.shape[2]
    scale = 1.0 / (occupied * count * lax.axis_size("chol"))
    full_green = lax.all_gather(green, "chol", axis=1, tiled=True)
    per_block = 4 if count % 4 == 0 else 1
    blocks = chol_vecs.reshape(count // per_block, per_block, occupied, basis)

    def step(carry, lblock):
        energy_acc, grad_acc = carry
        tmat = jnp.einsum("gip,wjp->wgij", lblock, full_green, preferred_element_type=jnp.float32)
        pairs = jnp.einsum("wgij,wgji->w", tmat, tmat)
        thalf = tmat.astype(jnp.bfloat16)
        gpart = jnp.einsum("wgki,gip->wkp", thalf, lblock, preferred_element_type=jnp.float32)
        return ((energy_acc + pairs, grad_acc + gpart), None)

    start = (jnp.zeros((walkers,), jnp.float32), jnp.zeros((walkers, occupied, basis), jnp.float32))
    (energy_part, grad_part), unused = lax.scan(step, start, blocks)
    energy_sum = lax.psum(energy_part, "chol")
    own_rows = lax.psum_scatter(grad_part, "chol", scatter_dimension=1, tiled=True)
    energy = -0.5 * scale * energy_sum
    grad_green = -scale * cotangent[:, None, None] * own_rows
    return (energy, grad_green)


def per_device(green, chol_vecs, cotangent):
    devices = lax.axis_size("chol")
    fits = (
        devices % (CORES * COLUMNS) == 0
        and devices > CORES * COLUMNS
        and green.shape[1] % 16 == 0
        and chol_vecs.shape[1] % 128 == 0
        and chol_vecs.shape[2] % 128 == 0
    )
    run = per_device_kernel if fits else per_device_plain
    return run(green, chol_vecs, cotangent)


def solution(mesh):
    placed = (P("groups", "chol", None), P("chol", None, None), P("groups"))
    return jax.shard_map(
        per_device,
        mesh=mesh,
        in_specs=placed,
        out_specs=(P("groups"), P("groups", "chol", None)),
        check_vma=False,
    )
```

```python
import functools

import jax
import jax.numpy as jnp
from jax import lax
from jax.experimental import pallas as pl
from jax.experimental.pallas import tpu as pltpu
from jax.sharding import PartitionSpec as P

CORES = 2
COLUMNS = 2


def exchange_kernel(
    scale,
    green_ref, chol_ref,
    energy_ref, grad_ref,
    vecs, full, half, partial, pair, ysend, yrecv, kept, zsend, zrecv, final,
    eparts, eyparts, ezparts, erecv_c, erecv_y, erecv_z,
    load_sem, own_sem, gz_send, gz_recv, gy_send, gy_recv, gc_send, gc_recv,
    rc_send, rc_recv, ry_send, ry_recv, rz_send, rz_recv,
    ec_sem, ey_sem, ez_send, ez_recv,
):
    walkers, rows, basis = green_ref.shape
    count, occupied, _ = chol_ref.shape
    planes = full.shape[1]
    bf16, f32 = jnp.bfloat16, jnp.float32

    me = lax.axis_index("chol")
    c = lax.rem(me, CORES)
    y = lax.rem(me // CORES, COLUMNS)
    z = me // (CORES * COLUMNS)

    def device(zz, yy, cc):
        return {"chol": (zz * COLUMNS + yy) * CORES + cc}

    plane = [lax.rem(z + k, planes) for k in range(planes)]
    source = [lax.rem(z - k + planes, planes) for k in range(planes)]
    over_z = [device(plane[k], y, c) for k in range(1, planes)]
    over_y = device(z, 1 - y, c)
    over_c = device(z, y, 1 - c)

    own = [pltpu.make_async_copy(green_ref.at[w], full.at[w, z, y, c], own_sem.at[w]) for w in range(walkers)]
    for copy in own:
        copy.start()
    loads = load_sem.shape[0]
    per = count // loads

    def load(i):
        return pltpu.make_async_copy(
            chol_ref.at[pl.ds(i * per, per)], vecs.at[pl.ds(i * per, per)], load_sem.at[i]
        )

    for i in range(loads):
        load(i).start()

    barrier = pltpu.get_barrier_semaphore()
    for peer in over_z + [over_y, over_c]:
        pl.semaphore_signal(barrier, inc=1, device_id=peer, device_id_type=pl.DeviceIdType.MESH)
    pl.semaphore_wait(barrier, planes + 1)

    def remote(src, dst, send_sem, recv_sem, peer):
        return pltpu.make_async_remote_copy(
            src_ref=src, dst_ref=dst, send_sem=send_sem, recv_sem=recv_sem,
            device_id=peer, device_id_type=pl.DeviceIdType.MESH,
        )

    def copy_gz(w, k):
        block = full.at[w, z, y, c]
        return remote(block, block, gz_send.at[w, k - 1], gz_recv.at[w, k - 1], over_z[k - 1])

    def copy_gy(w, k):
        block = full.at[w, source[k], y, c]
        return remote(block, block, gy_send.at[w, k], gy_recv.at[w, k], over_y)

    def copy_gc(w, k):
        column = full.at[w, :, y if k == 0 else 1 - y, c]
        return remote(column, column, gc_send.at[w, k], gc_recv.at[w, k], over_c)

    def copy_rc(w):
        return remote(partial.at[w, 1 - c], pair.at[w], rc_send.at[w], rc_recv.at[w], over_c)

    def copy_ry(w):
        return remote(ysend.at[w], yrecv.at[w], ry_send.at[w], ry_recv.at[w], over_y)

    def copy_rz(w, k):
        return remote(
            zsend.at[w, plane[k]], zrecv.at[w, k - 1], rz_send.at[w, k - 1], rz_recv.at[w, k - 1], over_z[k - 1]
        )

    def offer(w):
        pltpu.make_async_copy(green_ref.at[w], full.at[w, z, y, c], own_sem.at[w]).wait()
        for k in range(planes - 1, 0, -1):
            copy_gz(w, k).start()
        copy_gy(w, 0).start()

    def gather_z(w):
        for k in range(1, planes):
            copy_gz(w, k).wait_recv()
            copy_gy(w, k).start()
        copy_gc(w, 0).start()

    def gather_y(w):
        for k in range(planes):
            copy_gy(w, k).wait_recv()
        copy_gc(w, 1).start()

    def gather_c(w):
        for k in range(COLUMNS):
            copy_gc(w, k).wait_recv()

    def make_tmat(w):
        @pl.loop(0, loads)
        def _(i):
            first = i * per
            left = vecs[pl.ds(first, per)].reshape(per * occupied, basis)
            right = full[w].reshape(occupied, basis)
            tmat = lax.dot_general(left, right, (((1,), (1,)), ((), ())), preferred_element_type=f32)
            for j in range(per):
                at = pl.multiple_of((first + j) * occupied, occupied)
                half[:, pl.ds(at, occupied)] = tmat[j * occupied:(j + 1) * occupied].astype(bf16)

    chunk = 256 if basis % 256 == 0 else 128

    def make_grad(w):
        eparts[w] = jnp.zeros(eparts.shape[1:], f32)

        @pl.loop(0, basis // chunk)
        def _(i):
            at = pl.multiple_of(i * chunk, chunk)
            right = vecs[:, :, pl.ds(at, chunk)].reshape(count * occupied, chunk)
            part = jnp.dot(half[...], right, preferred_element_type=f32)
            green = full[w, :, :, :, :, pl.ds(at, chunk)].reshape(occupied, chunk)
            folded = (part * green.astype(f32)).reshape(occupied // 8, 8, chunk).sum(axis=0)
            for lane in range(0, chunk, 128):
                eparts[w] += folded[:, lane:lane + 128]
            for zz in range(planes):
                for yy in range(COLUMNS):
                    for cc in range(CORES):
                        row = ((zz * COLUMNS + yy) * CORES + cc) * rows
                        partial[w, cc, yy, zz, :, pl.ds(at, chunk)] = part[row:row + rows]

    def reduce_y(w):
        copy_rc(w).wait_recv()
        ysend[w] = (partial[w, c, 1 - y] + pair[w, 1 - y]).astype(bf16)
        copy_ry(w).start()
        kept[w] = partial[w, c, y] + pair[w, y]

    def reduce_z(w):
        copy_ry(w).wait_recv()
        zsend[w] = (kept[w] + yrecv[w].astype(f32)).astype(bf16)
        for k in range(planes - 1, 0, -1):
            copy_rz(w, k).start()
        final[w] = kept[w, z] + yrecv[w, z].astype(f32)

    def finish(w):
        total = final[w]
        for k in range(1, planes):
            copy_rz(w, k).wait_recv()
            total += zrecv[w, k - 1].astype(f32)
        grad_ref[w] = -scale * total

    last = walkers - 1
    for w in range(walkers):
        offer(w)
    gather_z(0)
    if walkers > 1:
        gather_z(1)
    gather_y(0)
    gather_c(0)
    for i in range(loads):
        load(i).wait()

    @pl.loop(0, walkers)
    def _(w):
        make_tmat(w)

        @pl.when(w > 0)
        def _():
            reduce_y(w - 1)

        @pl.when(w > 1)
        def _():
            finish(w - 2)

        @pl.when(w + 2 < walkers)
        def _():
            gather_z(w + 2)

        @pl.when(w + 1 < walkers)
        def _():
            gather_y(w + 1)

        make_grad(w)
        copy_rc(w).start()

        @pl.when(w > 0)
        def _():
            reduce_z(w - 1)

        @pl.when(w + 1 < walkers)
        def _():
            gather_c(w + 1)

    ec = remote(eparts, erecv_c, ec_sem.at[0], ec_sem.at[1], over_c)
    ec.start()
    ec.wait_recv()
    eyparts[...] = eparts[...] + erecv_c[...]
    ey = remote(eyparts, erecv_y, ey_sem.at[0], ey_sem.at[1], over_y)
    ey.start()
    reduce_y(last)
    if last > 0:
        finish(last - 1)
    ey.wait_recv()
    ezparts[...] = eyparts[...] + erecv_y[...]
    ez = [
        remote(ezparts, erecv_z.at[k - 1], ez_send.at[k - 1], ez_recv.at[k - 1], over_z[k - 1])
        for k in range(1, planes)
    ]
    for copy in ez:
        copy.start()
    reduce_z(last)
    esum = ezparts[...]
    for k in range(1, planes):
        ez[k - 1].wait_recv()
        esum += erecv_z[k - 1]
    for w in range(walkers):
        energy_ref[w] = -0.5 * scale * jnp.sum(esum[w])
    finish(last)
    for copy in [ec, ey] + ez:
        copy.wait_send()

    @pl.loop(0, walkers)
    def _(w):
        for k in range(1, planes):
            copy_gz(w, k).wait_send()
            copy_rz(w, k).wait_send()
        for k in range(planes):
            copy_gy(w, k).wait_send()
        for k in range(COLUMNS):
            copy_gc(w, k).wait_send()
        copy_rc(w).wait_send()
        copy_ry(w).wait_send()


def per_device_kernel(green, chol_vecs, cotangent):
    walkers, rows, basis = green.shape
    count, occupied, _ = chol_vecs.shape
    devices = lax.axis_size("chol")
    planes = devices // (CORES * COLUMNS)
    scale = 1.0 / (occupied * count * devices)
    per = max(i for i in (1, 2, 3) if count % i == 0)
    loads = count // per
    bf16, f32 = jnp.bfloat16, jnp.float32
    block = (rows, basis)
    dma = pltpu.SemaphoreType.DMA
    others = planes - 1
    estack = (walkers, 8, 128)
    energy, own_rows = pl.pallas_call(
        functools.partial(exchange_kernel, scale),
        out_shape=(
            jax.ShapeDtypeStruct((walkers,), f32),
            jax.ShapeDtypeStruct((walkers,) + block, f32),
        ),
        in_specs=[
            pl.BlockSpec(memory_space=pltpu.HBM),
            pl.BlockSpec(memory_space=pltpu.HBM),
        ],
        out_specs=(
            pl.BlockSpec(memory_space=pltpu.SMEM),
            pl.BlockSpec(memory_space=pltpu.VMEM),
        ),
        scratch_shapes=[
            pltpu.VMEM((count, occupied, basis), bf16),
            pltpu.VMEM((walkers, planes, COLUMNS, CORES) + block, bf16),
            pltpu.VMEM((occupied, count * occupied), bf16),
            pltpu.VMEM((walkers, CORES, COLUMNS, planes) + block, f32),
            pltpu.VMEM((walkers, COLUMNS, planes) + block, f32),
            pltpu.VMEM((walkers, planes) + block, bf16),
            pltpu.VMEM((walkers, planes) + block, bf16),
            pltpu.VMEM((walkers, planes) + block, f32),
            pltpu.VMEM((walkers, planes) + block, bf16),
            pltpu.VMEM((walkers, others) + block, bf16),
            pltpu.VMEM((walkers,) + block, f32),
            pltpu.VMEM(estack, f32),
            pltpu.VMEM(estack, f32),
            pltpu.VMEM(estack, f32),
            pltpu.VMEM(estack, f32),
            pltpu.VMEM(estack, f32),
            pltpu.VMEM((others,) + estack, f32),
            dma((loads,)), dma((walkers,)),
            dma((walkers, others)), dma((walkers, others)),
            dma((walkers, planes)), dma((walkers, planes)),
            dma((walkers, COLUMNS)), dma((walkers, COLUMNS)),
            dma((walkers,)), dma((walkers,)),
            dma((walkers,)), dma((walkers,)),
            dma((walkers, others)), dma((walkers, others)),
            dma((2,)), dma((2,)),
            dma((others,)), dma((others,)),
        ],
        compiler_params=pltpu.CompilerParams(
            collective_id=0, has_side_effects=True, vmem_limit_bytes=48 * 1024 * 1024
        ),
        cost_estimate=pl.CostEstimate(
            flops=4 * walkers * count * occupied * occupied * basis,
            bytes_accessed=2 * chol_vecs.size,
            transcendentals=0,
        ),
    )(green, chol_vecs)
    grad_green = cotangent[:, None, None] * own_rows
    return (energy, grad_green)


def per_device_plain(green, chol_vecs, cotangent):
    count = chol_vecs.shape[0]
    walkers = green.shape[0]
    occupied = chol_vecs.shape[1]
    basis = chol_vecs.shape[2]
    scale = 1.0 / (occupied * count * lax.axis_size("chol"))
    full_green = lax.all_gather(green, "chol", axis=1, tiled=True)
    per_block = 4 if count % 4 == 0 else 1
    blocks = chol_vecs.reshape(count // per_block, per_block, occupied, basis)

    def step(carry, lblock):
        energy_acc, grad_acc = carry
        tmat = jnp.einsum("gip,wjp->wgij", lblock, full_green, preferred_element_type=jnp.float32)
        pairs = jnp.einsum("wgij,wgji->w", tmat, tmat)
        thalf = tmat.astype(jnp.bfloat16)
        gpart = jnp.einsum("wgki,gip->wkp", thalf, lblock, preferred_element_type=jnp.float32)
        return ((energy_acc + pairs, grad_acc + gpart), None)

    start = (jnp.zeros((walkers,), jnp.float32), jnp.zeros((walkers, occupied, basis), jnp.float32))
    (energy_part, grad_part), unused = lax.scan(step, start, blocks)
    energy_sum = lax.psum(energy_part, "chol")
    own_rows = lax.psum_scatter(grad_part, "chol", scatter_dimension=1, tiled=True)
    energy = -0.5 * scale * energy_sum
    grad_green = -scale * cotangent[:, None, None] * own_rows
    return (energy, grad_green)


def per_device(green, chol_vecs, cotangent):
    devices = lax.axis_size("chol")
    fits = (
        devices % (CORES * COLUMNS) == 0
        and devices > CORES * COLUMNS
        and green.shape[1] % 16 == 0
        and chol_vecs.shape[1] % 128 == 0
        and chol_vecs.shape[2] % 128 == 0
    )
    run = per_device_kernel if fits else per_device_plain
    return run(green, chol_vecs, cotangent)


def solution(mesh):
    placed = (P("groups", "chol", None), P("chol", None, None), P("groups"))
    return jax.shard_map(
        per_device,
        mesh=mesh,
        in_specs=placed,
        out_specs=(P("groups"), P("groups", "chol", None)),
        check_vma=False,
    )
```

```python
import functools

import jax
import jax.numpy as jnp
from jax import lax
from jax.experimental import pallas as pl
from jax.experimental.pallas import tpu as pltpu
from jax.sharding import PartitionSpec as P

CORES = 2
COLUMNS = 2


def exchange_kernel(
    scale,
    green_ref, chol_ref,
    energy_ref, grad_ref,
    vecs, full, half, partial, pair, ysend, yrecv, kept, zsend, zrecv, final,
    eparts, eyparts, ezparts, erecv_c, erecv_y, erecv_z,
    load_sem, own_sem, gz_send, gz_recv, gy_send, gy_recv, gc_send, gc_recv,
    rc_send, rc_recv, ry_send, ry_recv, rz_send, rz_recv,
    ec_sem, ey_sem, ez_send, ez_recv,
):
    walkers, rows, basis = green_ref.shape
    count, occupied, _ = chol_ref.shape
    planes = full.shape[1]
    bf16, f32 = jnp.bfloat16, jnp.float32

    me = lax.axis_index("chol")
    c = lax.rem(me, CORES)
    y = lax.rem(me // CORES, COLUMNS)
    z = me // (CORES * COLUMNS)

    def device(zz, yy, cc):
        return {"chol": (zz * COLUMNS + yy) * CORES + cc}

    plane = [lax.rem(z + k, planes) for k in range(planes)]
    source = [lax.rem(z - k + planes, planes) for k in range(planes)]
    over_z = [device(plane[k], y, c) for k in range(1, planes)]
    over_y = device(z, 1 - y, c)
    over_c = device(z, y, 1 - c)

    own = [pltpu.make_async_copy(green_ref.at[w], full.at[w, z, y, c], own_sem.at[w]) for w in range(walkers)]
    for copy in own:
        copy.start()
    loads = load_sem.shape[0]
    per = count // loads

    def load(i):
        return pltpu.make_async_copy(
            chol_ref.at[pl.ds(i * per, per)], vecs.at[pl.ds(i * per, per)], load_sem.at[i]
        )

    for i in range(loads):
        load(i).start()

    barrier = pltpu.get_barrier_semaphore()
    for peer in over_z + [over_y, over_c]:
        pl.semaphore_signal(barrier, inc=1, device_id=peer, device_id_type=pl.DeviceIdType.MESH)
    pl.semaphore_wait(barrier, planes + 1)

    def remote(src, dst, send_sem, recv_sem, peer):
        return pltpu.make_async_remote_copy(
            src_ref=src, dst_ref=dst, send_sem=send_sem, recv_sem=recv_sem,
            device_id=peer, device_id_type=pl.DeviceIdType.MESH,
        )

    def copy_gz(w, k):
        block = full.at[w, z, y, c]
        return remote(block, block, gz_send.at[w, k - 1], gz_recv.at[w, k - 1], over_z[k - 1])

    def copy_gy(w, k):
        block = full.at[w, source[k], y, c]
        return remote(block, block, gy_send.at[w, k], gy_recv.at[w, k], over_y)

    def copy_gc(w, k):
        column = full.at[w, :, y if k == 0 else 1 - y, c]
        return remote(column, column, gc_send.at[w, k], gc_recv.at[w, k], over_c)

    def copy_rc(u):
        return remote(partial.at[u, 1 - c], pair.at[u], rc_send.at[u], rc_recv.at[u], over_c)

    def copy_ry(u):
        return remote(ysend.at[u], yrecv.at[u], ry_send.at[u], ry_recv.at[u], over_y)

    def copy_rz(u, k):
        return remote(
            zsend.at[u, plane[k]], zrecv.at[u, k - 1], rz_send.at[u, k - 1], rz_recv.at[u, k - 1], over_z[k - 1]
        )

    def offer(w):
        pltpu.make_async_copy(green_ref.at[w], full.at[w, z, y, c], own_sem.at[w]).wait()
        for k in range(planes - 1, 0, -1):
            copy_gz(w, k).start()
        copy_gy(w, 0).start()

    def gather_z(w):
        for k in range(1, planes):
            copy_gz(w, k).wait_recv()
            copy_gy(w, k).start()
        copy_gc(w, 0).start()

    def gather_y(w):
        for k in range(planes):
            copy_gy(w, k).wait_recv()
        copy_gc(w, 1).start()

    def gather_c(w):
        for k in range(COLUMNS):
            copy_gc(w, k).wait_recv()

    units, chunk = partial.shape[0], partial.shape[-1]
    chunks = basis // chunk
    period = loads + chunks

    def reduce_y(u):
        copy_rc(u).wait_recv()
        ysend[u] = (partial[u, c, 1 - y] + pair[u, 1 - y]).astype(bf16)
        copy_ry(u).start()
        kept[u] = partial[u, c, y] + pair[u, y]

    def reduce_z(u):
        copy_ry(u).wait_recv()
        zsend[u] = (kept[u] + yrecv[u].astype(f32)).astype(bf16)
        for k in range(planes - 1, 0, -1):
            copy_rz(u, k).start()
        final[u] = kept[u, z] + yrecv[u, z].astype(f32)

    def finish(u):
        total = final[u]
        for k in range(1, planes):
            copy_rz(u, k).wait_recv()
            total += zrecv[u, k - 1].astype(f32)
        at = pl.multiple_of(lax.rem(u, chunks) * chunk, chunk)
        grad_ref[u // chunks, :, pl.ds(at, chunk)] = -scale * total

    def service(tick):
        for lag, stage in ((2, reduce_y), (6, reduce_z), (10, finish)):
            made = tick - lag
            place = lax.rem(made + 2 * period, period) - loads
            unit = (made + 2 * period) // period * chunks - 2 * chunks + place

            @pl.when((place >= 0) & (unit >= 0) & (unit < units))
            def _():
                stage(unit)

    def make_tmat(w):
        @pl.loop(0, loads)
        def _(i):
            first = i * per
            left = vecs[pl.ds(first, per)].reshape(per * occupied, basis)
            right = full[w].reshape(occupied, basis)
            tmat = lax.dot_general(left, right, (((1,), (1,)), ((), ())), preferred_element_type=f32)
            for j in range(per):
                at = pl.multiple_of((first + j) * occupied, occupied)
                half[:, pl.ds(at, occupied)] = tmat[j * occupied:(j + 1) * occupied].astype(bf16)
            service(w * period + i)

    def make_grad(w):
        eparts[w] = jnp.zeros(eparts.shape[1:], f32)

        @pl.loop(0, chunks)
        def _(i):
            at = pl.multiple_of(i * chunk, chunk)
            right = vecs[:, :, pl.ds(at, chunk)].reshape(count * occupied, chunk)
            part = jnp.dot(half[...], right, preferred_element_type=f32)
            green = full[w, :, :, :, :, pl.ds(at, chunk)].reshape(occupied, chunk)
            folded = (part * green.astype(f32)).reshape(occupied // 8, 8, chunk).sum(axis=0)
            for lane in range(0, chunk, 128):
                eparts[w] += folded[:, lane:lane + 128]
            for zz in range(planes):
                for yy in range(COLUMNS):
                    for cc in range(CORES):
                        row = ((zz * COLUMNS + yy) * CORES + cc) * rows
                        partial[w * chunks + i, cc, yy, zz] = part[row:row + rows]
            copy_rc(w * chunks + i).start()
            service(w * period + loads + i)

    for w in range(walkers):
        offer(w)
    gather_z(0)
    gather_y(0)
    if walkers > 1:
        gather_z(1)
    gather_c(0)
    for i in range(loads):
        load(i).wait()

    @pl.loop(0, walkers)
    def _(w):
        make_tmat(w)

        @pl.when(w + 2 < walkers)
        def _():
            gather_z(w + 2)

        @pl.when(w + 1 < walkers)
        def _():
            gather_y(w + 1)

        make_grad(w)

        @pl.when(w + 1 < walkers)
        def _():
            gather_c(w + 1)

    end = walkers * period
    ec = remote(eparts, erecv_c, ec_sem.at[0], ec_sem.at[1], over_c)
    ec.start()

    @pl.loop(end, end + 2)
    def _(tick):
        service(tick)

    ec.wait_recv()
    eyparts[...] = eparts[...] + erecv_c[...]
    ey = remote(eyparts, erecv_y, ey_sem.at[0], ey_sem.at[1], over_y)
    ey.start()

    @pl.loop(end + 2, end + 6)
    def _(tick):
        service(tick)

    ey.wait_recv()
    ezparts[...] = eyparts[...] + erecv_y[...]
    ez = [
        remote(ezparts, erecv_z.at[k - 1], ez_send.at[k - 1], ez_recv.at[k - 1], over_z[k - 1])
        for k in range(1, planes)
    ]
    for copy in ez:
        copy.start()

    @pl.loop(end + 6, end + 10)
    def _(tick):
        service(tick)

    esum = ezparts[...]
    for k in range(1, planes):
        ez[k - 1].wait_recv()
        esum += erecv_z[k - 1]
    for w in range(walkers):
        energy_ref[w] = -0.5 * scale * jnp.sum(esum[w])
    for copy in [ec, ey] + ez:
        copy.wait_send()

    @pl.loop(0, walkers)
    def _(w):
        for k in range(1, planes):
            copy_gz(w, k).wait_send()
        for k in range(planes):
            copy_gy(w, k).wait_send()
        for k in range(COLUMNS):
            copy_gc(w, k).wait_send()

    @pl.loop(0, units)
    def _(u):
        copy_rc(u).wait_send()
        copy_ry(u).wait_send()
        for k in range(1, planes):
            copy_rz(u, k).wait_send()


def per_device_kernel(green, chol_vecs, cotangent):
    walkers, rows, basis = green.shape
    count, occupied, _ = chol_vecs.shape
    devices = lax.axis_size("chol")
    planes = devices // (CORES * COLUMNS)
    scale = 1.0 / (occupied * count * devices)
    per = max(i for i in (1, 2, 3) if count % i == 0)
    loads = count // per
    bf16, f32 = jnp.bfloat16, jnp.float32
    block = (rows, basis)
    chunk = 256 if basis % 256 == 0 else 128
    units = walkers * (basis // chunk)
    piece = (rows, chunk)
    dma = pltpu.SemaphoreType.DMA
    others = planes - 1
    estack = (walkers, 8, 128)
    energy, own_rows = pl.pallas_call(
        functools.partial(exchange_kernel, scale),
        out_shape=(
            jax.ShapeDtypeStruct((walkers,), f32),
            jax.ShapeDtypeStruct((walkers,) + block, f32),
        ),
        in_specs=[
            pl.BlockSpec(memory_space=pltpu.HBM),
            pl.BlockSpec(memory_space=pltpu.HBM),
        ],
        out_specs=(
            pl.BlockSpec(memory_space=pltpu.SMEM),
            pl.BlockSpec(memory_space=pltpu.VMEM),
        ),
        scratch_shapes=[
            pltpu.VMEM((count, occupied, basis), bf16),
            pltpu.VMEM((walkers, planes, COLUMNS, CORES) + block, bf16),
            pltpu.VMEM((occupied, count * occupied), bf16),
            pltpu.VMEM((units, CORES, COLUMNS, planes) + piece, f32),
            pltpu.VMEM((units, COLUMNS, planes) + piece, f32),
            pltpu.VMEM((units, planes) + piece, bf16),
            pltpu.VMEM((units, planes) + piece, bf16),
            pltpu.VMEM((units, planes) + piece, f32),
            pltpu.VMEM((units, planes) + piece, bf16),
            pltpu.VMEM((units, others) + piece, bf16),
            pltpu.VMEM((units,) + piece, f32),
            pltpu.VMEM(estack, f32),
            pltpu.VMEM(estack, f32),
            pltpu.VMEM(estack, f32),
            pltpu.VMEM(estack, f32),
            pltpu.VMEM(estack, f32),
            pltpu.VMEM((others,) + estack, f32),
            dma((loads,)), dma((walkers,)),
            dma((walkers, others)), dma((walkers, others)),
            dma((walkers, planes)), dma((walkers, planes)),
            dma((walkers, COLUMNS)), dma((walkers, COLUMNS)),
            dma((units,)), dma((units,)),
            dma((units,)), dma((units,)),
            dma((units, others)), dma((units, others)),
            dma((2,)), dma((2,)),
            dma((others,)), dma((others,)),
        ],
        compiler_params=pltpu.CompilerParams(
            collective_id=0, has_side_effects=True, vmem_limit_bytes=48 * 1024 * 1024
        ),
        cost_estimate=pl.CostEstimate(
            flops=4 * walkers * count * occupied * occupied * basis,
            bytes_accessed=2 * chol_vecs.size,
            transcendentals=0,
        ),
    )(green, chol_vecs)
    grad_green = cotangent[:, None, None] * own_rows
    return (energy, grad_green)


def per_device_plain(green, chol_vecs, cotangent):
    count = chol_vecs.shape[0]
    walkers = green.shape[0]
    occupied = chol_vecs.shape[1]
    basis = chol_vecs.shape[2]
    scale = 1.0 / (occupied * count * lax.axis_size("chol"))
    full_green = lax.all_gather(green, "chol", axis=1, tiled=True)
    per_block = 4 if count % 4 == 0 else 1
    blocks = chol_vecs.reshape(count // per_block, per_block, occupied, basis)

    def step(carry, lblock):
        energy_acc, grad_acc = carry
        tmat = jnp.einsum("gip,wjp->wgij", lblock, full_green, preferred_element_type=jnp.float32)
        pairs = jnp.einsum("wgij,wgji->w", tmat, tmat)
        thalf = tmat.astype(jnp.bfloat16)
        gpart = jnp.einsum("wgki,gip->wkp", thalf, lblock, preferred_element_type=jnp.float32)
        return ((energy_acc + pairs, grad_acc + gpart), None)

    start = (jnp.zeros((walkers,), jnp.float32), jnp.zeros((walkers, occupied, basis), jnp.float32))
    (energy_part, grad_part), unused = lax.scan(step, start, blocks)
    energy_sum = lax.psum(energy_part, "chol")
    own_rows = lax.psum_scatter(grad_part, "chol", scatter_dimension=1, tiled=True)
    energy = -0.5 * scale * energy_sum
    grad_green = -scale * cotangent[:, None, None] * own_rows
    return (energy, grad_green)


def per_device(green, chol_vecs, cotangent):
    devices = lax.axis_size("chol")
    fits = (
        devices % (CORES * COLUMNS) == 0
        and devices > CORES * COLUMNS
        and green.shape[1] % 16 == 0
        and chol_vecs.shape[1] % 128 == 0
        and chol_vecs.shape[2] % 128 == 0
    )
    run = per_device_kernel if fits else per_device_plain
    return run(green, chol_vecs, cotangent)


def solution(mesh):
    placed = (P("groups", "chol", None), P("chol", None, None), P("groups"))
    return jax.shard_map(
        per_device,
        mesh=mesh,
        in_specs=placed,
        out_specs=(P("groups"), P("groups", "chol", None)),
        check_vma=False,
    )
```

```python
import functools

import jax
import jax.numpy as jnp
from jax import lax
from jax.experimental import pallas as pl
from jax.experimental.pallas import tpu as pltpu
from jax.sharding import PartitionSpec as P

CORES = 2
COLUMNS = 2


def exchange_kernel(
    scale,
    green_ref, chol_ref,
    energy_ref, grad_ref,
    vecs, full, half, partial, pair, ysend, yrecv, kept, zsend, zrecv, final,
    eparts, eyparts, ezparts, erecv_c, erecv_y, erecv_z,
    load_sem, own_sem, gz_send, gz_recv, gy_send, gy_recv, gc_send, gc_recv,
    rc_send, rc_recv, ry_send, ry_recv, rz_send, rz_recv,
    ec_sem, ey_sem, ez_send, ez_recv,
):
    walkers, rows, basis = green_ref.shape
    count, occupied, _ = chol_ref.shape
    planes = full.shape[1]
    bf16, f32 = jnp.bfloat16, jnp.float32

    me = lax.axis_index("chol")
    c = lax.rem(me, CORES)
    y = lax.rem(me // CORES, COLUMNS)
    z = me // (CORES * COLUMNS)

    def device(zz, yy, cc):
        return {"chol": (zz * COLUMNS + yy) * CORES + cc}

    plane = [lax.rem(z + k, planes) for k in range(planes)]
    source = [lax.rem(z - k + planes, planes) for k in range(planes)]
    over_z = [device(plane[k], y, c) for k in range(1, planes)]
    over_y = device(z, 1 - y, c)
    over_c = device(z, y, 1 - c)

    own = [pltpu.make_async_copy(green_ref.at[w], full.at[w, z, y, c], own_sem.at[w]) for w in range(walkers)]
    for copy in own:
        copy.start()
    loads = load_sem.shape[0]
    per = count // loads

    def load(i):
        return pltpu.make_async_copy(
            chol_ref.at[pl.ds(i * per, per)], vecs.at[pl.ds(i * per, per)], load_sem.at[i]
        )

    for i in range(loads):
        load(i).start()

    barrier = pltpu.get_barrier_semaphore()
    for peer in over_z + [over_y, over_c]:
        pl.semaphore_signal(barrier, inc=1, device_id=peer, device_id_type=pl.DeviceIdType.MESH)
    pl.semaphore_wait(barrier, planes + 1)

    def remote(src, dst, send_sem, recv_sem, peer):
        return pltpu.make_async_remote_copy(
            src_ref=src, dst_ref=dst, send_sem=send_sem, recv_sem=recv_sem,
            device_id=peer, device_id_type=pl.DeviceIdType.MESH,
        )

    def copy_gz(w, k):
        block = full.at[w, z, y, c]
        return remote(block, block, gz_send.at[w, k - 1], gz_recv.at[w, k - 1], over_z[k - 1])

    def copy_gy(w, k):
        block = full.at[w, source[k], y, c]
        return remote(block, block, gy_send.at[w, k], gy_recv.at[w, k], over_y)

    def copy_gc(w, k):
        column = full.at[w, :, y if k == 0 else 1 - y, c]
        return remote(column, column, gc_send.at[w, k], gc_recv.at[w, k], over_c)

    def copy_rc(u):
        return remote(partial.at[u, 1 - c], pair.at[u], rc_send.at[u], rc_recv.at[u], over_c)

    def copy_ry(u):
        return remote(ysend.at[u], yrecv.at[u], ry_send.at[u], ry_recv.at[u], over_y)

    def copy_rz(u, k):
        return remote(
            zsend.at[u, plane[k]], zrecv.at[u, k - 1], rz_send.at[u, k - 1], rz_recv.at[u, k - 1], over_z[k - 1]
        )

    def offer(w):
        pltpu.make_async_copy(green_ref.at[w], full.at[w, z, y, c], own_sem.at[w]).wait()
        for k in range(planes - 1, 0, -1):
            copy_gz(w, k).start()
        copy_gy(w, 0).start()

    def gather_z(w):
        for k in range(1, planes):
            copy_gz(w, k).wait_recv()
            copy_gy(w, k).start()
        copy_gc(w, 0).start()

    def gather_y(w):
        for k in range(planes):
            copy_gy(w, k).wait_recv()
        copy_gc(w, 1).start()

    def gather_c(w):
        for k in range(COLUMNS):
            copy_gc(w, k).wait_recv()

    wide = half.shape[0]
    units, chunk = partial.shape[0], partial.shape[-1]
    chunks = basis // chunk
    split = 2 if chunks % 2 == 0 else 1
    steps = wide * chunks // split
    period = loads + steps
    lags = (1, 3, 5)

    def reduce_y(u):
        copy_rc(u).wait_recv()
        ysend[u] = (partial[u, c, 1 - y] + pair[u, 1 - y]).astype(bf16)
        copy_ry(u).start()
        kept[u] = partial[u, c, y] + pair[u, y]

    def reduce_z(u):
        copy_ry(u).wait_recv()
        zsend[u] = (kept[u] + yrecv[u].astype(f32)).astype(bf16)
        for k in range(planes - 1, 0, -1):
            copy_rz(u, k).start()
        final[u] = kept[u, z] + yrecv[u, z].astype(f32)

    def finish(u):
        total = final[u]
        for k in range(1, planes):
            copy_rz(u, k).wait_recv()
            total += zrecv[u, k - 1].astype(f32)
        at = pl.multiple_of(lax.rem(u, chunks) * chunk, chunk)
        grad_ref[u // chunks, :, pl.ds(at, chunk)] = -scale * total

    def service(tick):
        for lag, stage in zip(lags, (reduce_y, reduce_z, finish)):
            made = tick - lag + 2 * period
            place = lax.rem(made, period) - loads
            step = (made // period - 2) * steps + place

            @pl.when((place >= 0) & (step >= 0) & (step < units // split))
            def _():
                for j in range(split):
                    stage(step * split + j)

    def make_tmat(group):
        @pl.loop(0, loads)
        def _(i):
            first = i * per
            left = vecs[pl.ds(first, per)].reshape(per * occupied, basis)
            right = full[pl.ds(group * wide, wide)].reshape(wide * occupied, basis)
            tmat = lax.dot_general(left, right, (((1,), (1,)), ((), ())), preferred_element_type=f32)
            for j in range(per):
                at = pl.multiple_of((first + j) * occupied, occupied)
                for v in range(wide):
                    one = tmat[j * occupied:(j + 1) * occupied, v * occupied:(v + 1) * occupied]
                    half[v, :, pl.ds(at, occupied)] = one.astype(bf16)
            service(group * period + i)

    def make_grad(group):
        for v in range(wide):
            eparts[group * wide + v] = jnp.zeros(eparts.shape[1:], f32)

        @pl.loop(0, steps)
        def _(i):
            v = i * split // chunks
            w = group * wide + v
            size = split * chunk
            at = pl.multiple_of(lax.rem(i * split, chunks) * chunk, size)
            right = vecs[:, :, pl.ds(at, size)].reshape(count * occupied, size)
            part = jnp.dot(half[v], right, preferred_element_type=f32)
            green = full[w, :, :, :, :, pl.ds(at, size)].reshape(occupied, size)
            folded = (part * green.astype(f32)).reshape(occupied // 8, 8, size).sum(axis=0)
            eparts[w] += sum(folded[:, lane:lane + 128] for lane in range(0, size, 128))
            step = group * steps + i
            for j in range(split):
                for zz in range(planes):
                    for yy in range(COLUMNS):
                        for cc in range(CORES):
                            row = ((zz * COLUMNS + yy) * CORES + cc) * rows
                            partial[step * split + j, cc, yy, zz] = part[row:row + rows, j * chunk:(j + 1) * chunk]
                copy_rc(step * split + j).start()
            service(group * period + loads + i)

    for w in range(walkers):
        offer(w)
    for w in range(wide):
        gather_z(w)
    for w in range(wide):
        gather_y(w)
    for w in range(wide):
        gather_c(w)
    for i in range(loads):
        load(i).wait()
    groups = walkers // wide

    @pl.loop(0, groups)
    def _(group):
        make_tmat(group)

        @pl.when(group + 1 < groups)
        def _():
            for v in range(wide):
                gather_z((group + 1) * wide + v)
            for v in range(wide):
                gather_y((group + 1) * wide + v)

        make_grad(group)

        @pl.when(group + 1 < groups)
        def _():
            for v in range(wide):
                gather_c((group + 1) * wide + v)

    end = groups * period
    ec = remote(eparts, erecv_c, ec_sem.at[0], ec_sem.at[1], over_c)
    ec.start()

    @pl.loop(end, end + lags[0])
    def _(tick):
        service(tick)

    ec.wait_recv()
    eyparts[...] = eparts[...] + erecv_c[...]
    ey = remote(eyparts, erecv_y, ey_sem.at[0], ey_sem.at[1], over_y)
    ey.start()

    @pl.loop(end + lags[0], end + lags[1])
    def _(tick):
        service(tick)

    ey.wait_recv()
    ezparts[...] = eyparts[...] + erecv_y[...]
    ez = [
        remote(ezparts, erecv_z.at[k - 1], ez_send.at[k - 1], ez_recv.at[k - 1], over_z[k - 1])
        for k in range(1, planes)
    ]
    for copy in ez:
        copy.start()

    @pl.loop(end + lags[1], end + lags[2])
    def _(tick):
        service(tick)

    esum = ezparts[...]
    for k in range(1, planes):
        ez[k - 1].wait_recv()
        esum += erecv_z[k - 1]
    for w in range(walkers):
        energy_ref[w] = -0.5 * scale * jnp.sum(esum[w])
    for copy in [ec, ey] + ez:
        copy.wait_send()

    @pl.loop(0, walkers)
    def _(w):
        for k in range(1, planes):
            copy_gz(w, k).wait_send()
        for k in range(planes):
            copy_gy(w, k).wait_send()
        for k in range(COLUMNS):
            copy_gc(w, k).wait_send()

    @pl.loop(0, units)
    def _(u):
        copy_rc(u).wait_send()
        copy_ry(u).wait_send()
        for k in range(1, planes):
            copy_rz(u, k).wait_send()


def per_device_kernel(green, chol_vecs, cotangent):
    walkers, rows, basis = green.shape
    count, occupied, _ = chol_vecs.shape
    devices = lax.axis_size("chol")
    planes = devices // (CORES * COLUMNS)
    scale = 1.0 / (occupied * count * devices)
    per = max(i for i in (1, 2, 3) if count % i == 0)
    loads = count // per
    bf16, f32 = jnp.bfloat16, jnp.float32
    block = (rows, basis)
    chunk = 256 if basis % 256 == 0 else 128
    units = walkers * (basis // chunk)
    wide = 2 if walkers % 2 == 0 else 1
    piece = (rows, chunk)
    dma = pltpu.SemaphoreType.DMA
    others = planes - 1
    estack = (walkers, 8, 128)
    energy, own_rows = pl.pallas_call(
        functools.partial(exchange_kernel, scale),
        out_shape=(
            jax.ShapeDtypeStruct((walkers,), f32),
            jax.ShapeDtypeStruct((walkers,) + block, f32),
        ),
        in_specs=[
            pl.BlockSpec(memory_space=pltpu.HBM),
            pl.BlockSpec(memory_space=pltpu.HBM),
        ],
        out_specs=(
            pl.BlockSpec(memory_space=pltpu.SMEM),
            pl.BlockSpec(memory_space=pltpu.VMEM),
        ),
        scratch_shapes=[
            pltpu.VMEM((count, occupied, basis), bf16),
            pltpu.VMEM((walkers, planes, COLUMNS, CORES) + block, bf16),
            pltpu.VMEM((wide, occupied, count * occupied), bf16),
            pltpu.VMEM((units, CORES, COLUMNS, planes) + piece, f32),
            pltpu.VMEM((units, COLUMNS, planes) + piece, f32),
            pltpu.VMEM((units, planes) + piece, bf16),
            pltpu.VMEM((units, planes) + piece, bf16),
            pltpu.VMEM((units, planes) + piece, f32),
            pltpu.VMEM((units, planes) + piece, bf16),
            pltpu.VMEM((units, others) + piece, bf16),
            pltpu.VMEM((units,) + piece, f32),
            pltpu.VMEM(estack, f32),
            pltpu.VMEM(estack, f32),
            pltpu.VMEM(estack, f32),
            pltpu.VMEM(estack, f32),
            pltpu.VMEM(estack, f32),
            pltpu.VMEM((others,) + estack, f32),
            dma((loads,)), dma((walkers,)),
            dma((walkers, others)), dma((walkers, others)),
            dma((walkers, planes)), dma((walkers, planes)),
            dma((walkers, COLUMNS)), dma((walkers, COLUMNS)),
            dma((units,)), dma((units,)),
            dma((units,)), dma((units,)),
            dma((units, others)), dma((units, others)),
            dma((2,)), dma((2,)),
            dma((others,)), dma((others,)),
        ],
        compiler_params=pltpu.CompilerParams(
            collective_id=0, has_side_effects=True, vmem_limit_bytes=48 * 1024 * 1024
        ),
        cost_estimate=pl.CostEstimate(
            flops=4 * walkers * count * occupied * occupied * basis,
            bytes_accessed=2 * chol_vecs.size,
            transcendentals=0,
        ),
    )(green, chol_vecs)
    grad_green = cotangent[:, None, None] * own_rows
    return (energy, grad_green)


def per_device_plain(green, chol_vecs, cotangent):
    count = chol_vecs.shape[0]
    walkers = green.shape[0]
    occupied = chol_vecs.shape[1]
    basis = chol_vecs.shape[2]
    scale = 1.0 / (occupied * count * lax.axis_size("chol"))
    full_green = lax.all_gather(green, "chol", axis=1, tiled=True)
    per_block = 4 if count % 4 == 0 else 1
    blocks = chol_vecs.reshape(count // per_block, per_block, occupied, basis)

    def step(carry, lblock):
        energy_acc, grad_acc = carry
        tmat = jnp.einsum("gip,wjp->wgij", lblock, full_green, preferred_element_type=jnp.float32)
        pairs = jnp.einsum("wgij,wgji->w", tmat, tmat)
        thalf = tmat.astype(jnp.bfloat16)
        gpart = jnp.einsum("wgki,gip->wkp", thalf, lblock, preferred_element_type=jnp.float32)
        return ((energy_acc + pairs, grad_acc + gpart), None)

    start = (jnp.zeros((walkers,), jnp.float32), jnp.zeros((walkers, occupied, basis), jnp.float32))
    (energy_part, grad_part), unused = lax.scan(step, start, blocks)
    energy_sum = lax.psum(energy_part, "chol")
    own_rows = lax.psum_scatter(grad_part, "chol", scatter_dimension=1, tiled=True)
    energy = -0.5 * scale * energy_sum
    grad_green = -scale * cotangent[:, None, None] * own_rows
    return (energy, grad_green)


def per_device(green, chol_vecs, cotangent):
    devices = lax.axis_size("chol")
    fits = (
        devices % (CORES * COLUMNS) == 0
        and devices > CORES * COLUMNS
        and green.shape[1] % 16 == 0
        and chol_vecs.shape[1] % 128 == 0
        and chol_vecs.shape[2] % 128 == 0
    )
    run = per_device_kernel if fits else per_device_plain
    return run(green, chol_vecs, cotangent)


def solution(mesh):
    placed = (P("groups", "chol", None), P("chol", None, None), P("groups"))
    return jax.shard_map(
        per_device,
        mesh=mesh,
        in_specs=placed,
        out_specs=(P("groups"), P("groups", "chol", None)),
        check_vma=False,
    )
```

```python
import functools

import jax
import jax.numpy as jnp
from jax import lax
from jax.experimental import pallas as pl
from jax.experimental.pallas import tpu as pltpu
from jax.sharding import PartitionSpec as P

CORES = 2
COLUMNS = 2


def exchange_kernel(
    scale,
    green_ref, chol_ref,
    energy_ref, grad_ref,
    vecs, full, turned, half, partial, pair, ysend, yrecv, kept, zsend, zrecv, final,
    eparts, eyparts, ezparts, erecv_c, erecv_y, erecv_z,
    load_sem, own_sem, gz_send, gz_recv, gy_send, gy_recv, gc_send, gc_recv,
    rc_send, rc_recv, ry_send, ry_recv, rz_send, rz_recv,
    ec_sem, ey_sem, ez_send, ez_recv,
):
    walkers, rows, basis = green_ref.shape
    count, occupied, _ = chol_ref.shape
    planes = full.shape[1]
    bf16, f32 = jnp.bfloat16, jnp.float32

    me = lax.axis_index("chol")
    c = lax.rem(me, CORES)
    y = lax.rem(me // CORES, COLUMNS)
    z = me // (CORES * COLUMNS)

    def device(zz, yy, cc):
        return {"chol": (zz * COLUMNS + yy) * CORES + cc}

    plane = [lax.rem(z + k, planes) for k in range(planes)]
    source = [lax.rem(z - k + planes, planes) for k in range(planes)]
    over_z = [device(plane[k], y, c) for k in range(1, planes)]
    over_y = device(z, 1 - y, c)
    over_c = device(z, y, 1 - c)

    own = [pltpu.make_async_copy(green_ref.at[w], full.at[w, z, y, c], own_sem.at[w]) for w in range(walkers)]
    for copy in own:
        copy.start()
    loads = load_sem.shape[0]
    per = count // loads

    def load(i):
        return pltpu.make_async_copy(
            chol_ref.at[pl.ds(i * per, per)], vecs.at[pl.ds(i * per, per)], load_sem.at[i]
        )

    for i in range(loads):
        load(i).start()

    barrier = pltpu.get_barrier_semaphore()
    for peer in over_z + [over_y, over_c]:
        pl.semaphore_signal(barrier, inc=1, device_id=peer, device_id_type=pl.DeviceIdType.MESH)
    pl.semaphore_wait(barrier, planes + 1)

    def remote(src, dst, send_sem, recv_sem, peer):
        return pltpu.make_async_remote_copy(
            src_ref=src, dst_ref=dst, send_sem=send_sem, recv_sem=recv_sem,
            device_id=peer, device_id_type=pl.DeviceIdType.MESH,
        )

    def copy_gz(w, k):
        block = full.at[w, z, y, c]
        return remote(block, block, gz_send.at[w, k - 1], gz_recv.at[w, k - 1], over_z[k - 1])

    def copy_gy(w, k):
        block = full.at[w, source[k], y, c]
        return remote(block, block, gy_send.at[w, k], gy_recv.at[w, k], over_y)

    def copy_gc(w, k):
        column = full.at[w, :, y if k == 0 else 1 - y, c]
        return remote(column, column, gc_send.at[w, k], gc_recv.at[w, k], over_c)

    def copy_rc(u):
        return remote(partial.at[u, 1 - c], pair.at[u], rc_send.at[u], rc_recv.at[u], over_c)

    def copy_ry(u):
        return remote(ysend.at[u], yrecv.at[u], ry_send.at[u], ry_recv.at[u], over_y)

    def copy_rz(u, k):
        return remote(
            zsend.at[u, plane[k]], zrecv.at[u, k - 1], rz_send.at[u, k - 1], rz_recv.at[u, k - 1], over_z[k - 1]
        )

    def offer(w):
        pltpu.make_async_copy(green_ref.at[w], full.at[w, z, y, c], own_sem.at[w]).wait()
        for k in range(planes - 1, 0, -1):
            copy_gz(w, k).start()
        copy_gy(w, 0).start()

    def gather_z(w):
        for k in range(1, planes):
            copy_gz(w, k).wait_recv()
            copy_gy(w, k).start()
        copy_gc(w, 0).start()

    def gather_y(w):
        for k in range(planes):
            copy_gy(w, k).wait_recv()
        copy_gc(w, 1).start()

    def gather_c(w):
        for k in range(COLUMNS):
            copy_gc(w, k).wait_recv()

    units, chunk = partial.shape[0], partial.shape[-1]
    chunks = basis // chunk
    period = loads + chunks

    def reduce_y(u):
        copy_rc(u).wait_recv()
        ysend[u] = (partial[u, c, 1 - y] + pair[u, 1 - y]).astype(bf16)
        copy_ry(u).start()
        kept[u] = partial[u, c, y] + pair[u, y]

    def reduce_z(u):
        copy_ry(u).wait_recv()
        zsend[u] = (kept[u] + yrecv[u].astype(f32)).astype(bf16)
        for k in range(planes - 1, 0, -1):
            copy_rz(u, k).start()
        final[u] = kept[u, z] + yrecv[u, z].astype(f32)

    def finish(u):
        total = final[u]
        for k in range(1, planes):
            copy_rz(u, k).wait_recv()
            total += zrecv[u, k - 1].astype(f32)
        at = pl.multiple_of(lax.rem(u, chunks) * chunk, chunk)
        grad_ref[u // chunks, :, pl.ds(at, chunk)] = -scale * total

    def service(tick):
        for lag, stage in ((2, reduce_y), (6, reduce_z), (10, finish)):
            made = tick - lag
            place = lax.rem(made + 2 * period, period) - loads
            unit = (made + 2 * period) // period * chunks - 2 * chunks + place

            @pl.when((place >= 0) & (unit >= 0) & (unit < units))
            def _():
                stage(unit)

    def make_tmat(w):
        turned[...] = full[w].reshape(occupied, basis).T

        @pl.loop(0, loads)
        def _(i):
            first = i * per
            left = vecs[pl.ds(first, per)].reshape(per * occupied, basis)
            tmat = jnp.dot(left, turned[...], preferred_element_type=f32)
            for j in range(per):
                at = pl.multiple_of((first + j) * occupied, occupied)
                half[:, pl.ds(at, occupied)] = tmat[j * occupied:(j + 1) * occupied].astype(bf16)
            service(w * period + i)

    def make_grad(w):
        eparts[w] = jnp.zeros(eparts.shape[1:], f32)

        @pl.loop(0, chunks)
        def _(i):
            at = pl.multiple_of(i * chunk, chunk)
            right = vecs[:, :, pl.ds(at, chunk)].reshape(count * occupied, chunk)
            part = jnp.dot(half[...], right, preferred_element_type=f32)
            green = full[w, :, :, :, :, pl.ds(at, chunk)].reshape(occupied, chunk)
            folded = (part * green.astype(f32)).reshape(occupied // 8, 8, chunk).sum(axis=0)
            for lane in range(0, chunk, 128):
                eparts[w] += folded[:, lane:lane + 128]
            for zz in range(planes):
                for yy in range(COLUMNS):
                    for cc in range(CORES):
                        row = ((zz * COLUMNS + yy) * CORES + cc) * rows
                        partial[w * chunks + i, cc, yy, zz] = part[row:row + rows]
            copy_rc(w * chunks + i).start()
            service(w * period + loads + i)

    for w in range(walkers):
        offer(w)
    gather_z(0)
    gather_y(0)
    if walkers > 1:
        gather_z(1)
    gather_c(0)
    for i in range(loads):
        load(i).wait()

    @pl.loop(0, walkers)
    def _(w):
        make_tmat(w)

        @pl.when(w + 2 < walkers)
        def _():
            gather_z(w + 2)

        @pl.when(w + 1 < walkers)
        def _():
            gather_y(w + 1)

        make_grad(w)

        @pl.when(w + 1 < walkers)
        def _():
            gather_c(w + 1)

    end = walkers * period
    ec = remote(eparts, erecv_c, ec_sem.at[0], ec_sem.at[1], over_c)
    ec.start()

    @pl.loop(end, end + 2)
    def _(tick):
        service(tick)

    ec.wait_recv()
    eyparts[...] = eparts[...] + erecv_c[...]
    ey = remote(eyparts, erecv_y, ey_sem.at[0], ey_sem.at[1], over_y)
    ey.start()

    @pl.loop(end + 2, end + 6)
    def _(tick):
        service(tick)

    ey.wait_recv()
    ezparts[...] = eyparts[...] + erecv_y[...]
    ez = [
        remote(ezparts, erecv_z.at[k - 1], ez_send.at[k - 1], ez_recv.at[k - 1], over_z[k - 1])
        for k in range(1, planes)
    ]
    for copy in ez:
        copy.start()

    @pl.loop(end + 6, end + 10)
    def _(tick):
        service(tick)

    esum = ezparts[...]
    for k in range(1, planes):
        ez[k - 1].wait_recv()
        esum += erecv_z[k - 1]
    for w in range(walkers):
        energy_ref[w] = -0.5 * scale * jnp.sum(esum[w])
    for copy in [ec, ey] + ez:
        copy.wait_send()

    @pl.loop(0, walkers)
    def _(w):
        for k in range(1, planes):
            copy_gz(w, k).wait_send()
        for k in range(planes):
            copy_gy(w, k).wait_send()
        for k in range(COLUMNS):
            copy_gc(w, k).wait_send()

    @pl.loop(0, units)
    def _(u):
        copy_rc(u).wait_send()
        copy_ry(u).wait_send()
        for k in range(1, planes):
            copy_rz(u, k).wait_send()


def per_device_kernel(green, chol_vecs, cotangent):
    walkers, rows, basis = green.shape
    count, occupied, _ = chol_vecs.shape
    devices = lax.axis_size("chol")
    planes = devices // (CORES * COLUMNS)
    scale = 1.0 / (occupied * count * devices)
    per = max(i for i in (1, 2, 3) if count % i == 0)
    loads = count // per
    bf16, f32 = jnp.bfloat16, jnp.float32
    block = (rows, basis)
    chunk = 256 if basis % 256 == 0 else 128
    units = walkers * (basis // chunk)
    piece = (rows, chunk)
    dma = pltpu.SemaphoreType.DMA
    others = planes - 1
    estack = (walkers, 8, 128)
    energy, own_rows = pl.pallas_call(
        functools.partial(exchange_kernel, scale),
        out_shape=(
            jax.ShapeDtypeStruct((walkers,), f32),
            jax.ShapeDtypeStruct((walkers,) + block, f32),
        ),
        in_specs=[
            pl.BlockSpec(memory_space=pltpu.HBM),
            pl.BlockSpec(memory_space=pltpu.HBM),
        ],
        out_specs=(
            pl.BlockSpec(memory_space=pltpu.SMEM),
            pl.BlockSpec(memory_space=pltpu.VMEM),
        ),
        scratch_shapes=[
            pltpu.VMEM((count, occupied, basis), bf16),
            pltpu.VMEM((walkers, planes, COLUMNS, CORES) + block, bf16),
            pltpu.VMEM((basis, occupied), bf16),
            pltpu.VMEM((occupied, count * occupied), bf16),
            pltpu.VMEM((units, CORES, COLUMNS, planes) + piece, f32),
            pltpu.VMEM((units, COLUMNS, planes) + piece, f32),
            pltpu.VMEM((units, planes) + piece, bf16),
            pltpu.VMEM((units, planes) + piece, bf16),
            pltpu.VMEM((units, planes) + piece, f32),
            pltpu.VMEM((units, planes) + piece, bf16),
            pltpu.VMEM((units, others) + piece, bf16),
            pltpu.VMEM((units,) + piece, f32),
            pltpu.VMEM(estack, f32),
            pltpu.VMEM(estack, f32),
            pltpu.VMEM(estack, f32),
            pltpu.VMEM(estack, f32),
            pltpu.VMEM(estack, f32),
            pltpu.VMEM((others,) + estack, f32),
            dma((loads,)), dma((walkers,)),
            dma((walkers, others)), dma((walkers, others)),
            dma((walkers, planes)), dma((walkers, planes)),
            dma((walkers, COLUMNS)), dma((walkers, COLUMNS)),
            dma((units,)), dma((units,)),
            dma((units,)), dma((units,)),
            dma((units, others)), dma((units, others)),
            dma((2,)), dma((2,)),
            dma((others,)), dma((others,)),
        ],
        compiler_params=pltpu.CompilerParams(
            collective_id=0, has_side_effects=True, vmem_limit_bytes=48 * 1024 * 1024
        ),
        cost_estimate=pl.CostEstimate(
            flops=4 * walkers * count * occupied * occupied * basis,
            bytes_accessed=2 * chol_vecs.size,
            transcendentals=0,
        ),
    )(green, chol_vecs)
    grad_green = cotangent[:, None, None] * own_rows
    return (energy, grad_green)


def per_device_plain(green, chol_vecs, cotangent):
    count = chol_vecs.shape[0]
    walkers = green.shape[0]
    occupied = chol_vecs.shape[1]
    basis = chol_vecs.shape[2]
    scale = 1.0 / (occupied * count * lax.axis_size("chol"))
    full_green = lax.all_gather(green, "chol", axis=1, tiled=True)
    per_block = 4 if count % 4 == 0 else 1
    blocks = chol_vecs.reshape(count // per_block, per_block, occupied, basis)

    def step(carry, lblock):
        energy_acc, grad_acc = carry
        tmat = jnp.einsum("gip,wjp->wgij", lblock, full_green, preferred_element_type=jnp.float32)
        pairs = jnp.einsum("wgij,wgji->w", tmat, tmat)
        thalf = tmat.astype(jnp.bfloat16)
        gpart = jnp.einsum("wgki,gip->wkp", thalf, lblock, preferred_element_type=jnp.float32)
        return ((energy_acc + pairs, grad_acc + gpart), None)

    start = (jnp.zeros((walkers,), jnp.float32), jnp.zeros((walkers, occupied, basis), jnp.float32))
    (energy_part, grad_part), unused = lax.scan(step, start, blocks)
    energy_sum = lax.psum(energy_part, "chol")
    own_rows = lax.psum_scatter(grad_part, "chol", scatter_dimension=1, tiled=True)
    energy = -0.5 * scale * energy_sum
    grad_green = -scale * cotangent[:, None, None] * own_rows
    return (energy, grad_green)


def per_device(green, chol_vecs, cotangent):
    devices = lax.axis_size("chol")
    fits = (
        devices % (CORES * COLUMNS) == 0
        and devices > CORES * COLUMNS
        and green.shape[1] % 16 == 0
        and chol_vecs.shape[1] % 128 == 0
        and chol_vecs.shape[2] % 128 == 0
    )
    run = per_device_kernel if fits else per_device_plain
    return run(green, chol_vecs, cotangent)


def solution(mesh):
    placed = (P("groups", "chol", None), P("chol", None, None), P("groups"))
    return jax.shard_map(
        per_device,
        mesh=mesh,
        in_specs=placed,
        out_specs=(P("groups"), P("groups", "chol", None)),
        check_vma=False,
    )
```

```python
import functools

import jax
import jax.numpy as jnp
from jax import lax
from jax.experimental import pallas as pl
from jax.experimental.pallas import tpu as pltpu
from jax.sharding import PartitionSpec as P

CORES = 2
COLUMNS = 2


def exchange_kernel(
    scale,
    green_ref, chol_ref,
    energy_ref, grad_ref,
    vecs, full, half, partial, csend, pair, ysend, yrecv, kept, zsend, zrecv, final,
    eparts, eyparts, ezparts, erecv_c, erecv_y, erecv_z,
    load_sem, own_sem, gz_send, gz_recv, gy_send, gy_recv, gc_send, gc_recv,
    rc_send, rc_recv, ry_send, ry_recv, rz_send, rz_recv,
    ec_sem, ey_sem, ez_send, ez_recv,
):
    walkers, rows, basis = green_ref.shape
    count, occupied, _ = chol_ref.shape
    planes = full.shape[1]
    bf16, f32 = jnp.bfloat16, jnp.float32

    me = lax.axis_index("chol")
    c = lax.rem(me, CORES)
    y = lax.rem(me // CORES, COLUMNS)
    z = me // (CORES * COLUMNS)

    def device(zz, yy, cc):
        return {"chol": (zz * COLUMNS + yy) * CORES + cc}

    plane = [lax.rem(z + k, planes) for k in range(planes)]
    source = [lax.rem(z - k + planes, planes) for k in range(planes)]
    over_z = [device(plane[k], y, c) for k in range(1, planes)]
    over_y = device(z, 1 - y, c)
    over_c = device(z, y, 1 - c)

    own = [pltpu.make_async_copy(green_ref.at[w], full.at[w, z, y, c], own_sem.at[w]) for w in range(walkers)]
    for copy in own:
        copy.start()
    loads = load_sem.shape[0]
    per = count // loads

    def load(i):
        return pltpu.make_async_copy(
            chol_ref.at[pl.ds(i * per, per)], vecs.at[pl.ds(i * per, per)], load_sem.at[i]
        )

    for i in range(loads):
        load(i).start()

    barrier = pltpu.get_barrier_semaphore()
    for peer in over_z + [over_y, over_c]:
        pl.semaphore_signal(barrier, inc=1, device_id=peer, device_id_type=pl.DeviceIdType.MESH)
    pl.semaphore_wait(barrier, planes + 1)

    def remote(src, dst, send_sem, recv_sem, peer):
        return pltpu.make_async_remote_copy(
            src_ref=src, dst_ref=dst, send_sem=send_sem, recv_sem=recv_sem,
            device_id=peer, device_id_type=pl.DeviceIdType.MESH,
        )

    def copy_gz(w, k):
        block = full.at[w, z, y, c]
        return remote(block, block, gz_send.at[w, k - 1], gz_recv.at[w, k - 1], over_z[k - 1])

    def copy_gy(w, k):
        block = full.at[w, source[k], y, c]
        return remote(block, block, gy_send.at[w, k], gy_recv.at[w, k], over_y)

    def copy_gc(w, k):
        column = full.at[w, :, y if k == 0 else 1 - y, c]
        return remote(column, column, gc_send.at[w, k], gc_recv.at[w, k], over_c)

    def copy_rc(u):
        return remote(csend.at[u, 1 - c], pair.at[u], rc_send.at[u], rc_recv.at[u], over_c)

    def copy_ry(u):
        return remote(ysend.at[u], yrecv.at[u], ry_send.at[u], ry_recv.at[u], over_y)

    def copy_rz(u, k):
        return remote(
            zsend.at[u, plane[k]], zrecv.at[u, k - 1], rz_send.at[u, k - 1], rz_recv.at[u, k - 1], over_z[k - 1]
        )

    def offer(w):
        pltpu.make_async_copy(green_ref.at[w], full.at[w, z, y, c], own_sem.at[w]).wait()
        for k in range(planes - 1, 0, -1):
            copy_gz(w, k).start()
        copy_gy(w, 0).start()

    def gather_z(w):
        for k in range(1, planes):
            copy_gz(w, k).wait_recv()
            copy_gy(w, k).start()
        copy_gc(w, 0).start()

    def gather_y(w):
        for k in range(planes):
            copy_gy(w, k).wait_recv()
        copy_gc(w, 1).start()

    def gather_c(w):
        for k in range(COLUMNS):
            copy_gc(w, k).wait_recv()

    units, chunk = partial.shape[0], partial.shape[-1]
    chunks = basis // chunk
    period = loads + chunks

    def reduce_y(u):
        copy_rc(u).wait_recv()
        ysend[u] = (partial[u, c, 1 - y] + pair[u, 1 - y].astype(f32)).astype(bf16)
        copy_ry(u).start()
        kept[u] = partial[u, c, y] + pair[u, y].astype(f32)

    def reduce_z(u):
        copy_ry(u).wait_recv()
        zsend[u] = (kept[u] + yrecv[u].astype(f32)).astype(bf16)
        for k in range(planes - 1, 0, -1):
            copy_rz(u, k).start()
        final[u] = kept[u, z] + yrecv[u, z].astype(f32)

    def finish(u):
        total = final[u]
        for k in range(1, planes):
            copy_rz(u, k).wait_recv()
            total += zrecv[u, k - 1].astype(f32)
        at = pl.multiple_of(lax.rem(u, chunks) * chunk, chunk)
        grad_ref[u // chunks, :, pl.ds(at, chunk)] = -scale * total

    def service(tick):
        for lag, stage in ((2, reduce_y), (6, reduce_z), (10, finish)):
            made = tick - lag
            place = lax.rem(made + 2 * period, period) - loads
            unit = (made + 2 * period) // period * chunks - 2 * chunks + place

            @pl.when((place >= 0) & (unit >= 0) & (unit < units))
            def _():
                stage(unit)

    def make_tmat(w):
        @pl.loop(0, loads)
        def _(i):
            first = i * per
            left = vecs[pl.ds(first, per)].reshape(per * occupied, basis)
            right = full[w].reshape(occupied, basis)
            tmat = lax.dot_general(left, right, (((1,), (1,)), ((), ())), preferred_element_type=f32)
            for j in range(per):
                at = pl.multiple_of((first + j) * occupied, occupied)
                half[:, pl.ds(at, occupied)] = tmat[j * occupied:(j + 1) * occupied].astype(bf16)
            service(w * period + i)

    def make_grad(w):
        eparts[w] = jnp.zeros(eparts.shape[1:], f32)

        @pl.loop(0, chunks)
        def _(i):
            at = pl.multiple_of(i * chunk, chunk)
            right = vecs[:, :, pl.ds(at, chunk)].reshape(count * occupied, chunk)
            part = jnp.dot(half[...], right, preferred_element_type=f32)
            green = full[w, :, :, :, :, pl.ds(at, chunk)].reshape(occupied, chunk)
            folded = (part * green.astype(f32)).reshape(occupied // 8, 8, chunk).sum(axis=0)
            for lane in range(0, chunk, 128):
                eparts[w] += folded[:, lane:lane + 128]
            for zz in range(planes):
                for yy in range(COLUMNS):
                    for cc in range(CORES):
                        row = ((zz * COLUMNS + yy) * CORES + cc) * rows
                        partial[w * chunks + i, cc, yy, zz] = part[row:row + rows]
                        csend[w * chunks + i, cc, yy, zz] = part[row:row + rows].astype(bf16)
            copy_rc(w * chunks + i).start()
            service(w * period + loads + i)

    for w in range(walkers):
        offer(w)
    gather_z(0)
    gather_y(0)
    if walkers > 1:
        gather_z(1)
    gather_c(0)
    for i in range(loads):
        load(i).wait()

    @pl.loop(0, walkers)
    def _(w):
        make_tmat(w)

        @pl.when(w + 2 < walkers)
        def _():
            gather_z(w + 2)

        @pl.when(w + 1 < walkers)
        def _():
            gather_y(w + 1)

        make_grad(w)

        @pl.when(w + 1 < walkers)
        def _():
            gather_c(w + 1)

    end = walkers * period
    ec = remote(eparts, erecv_c, ec_sem.at[0], ec_sem.at[1], over_c)
    ec.start()

    @pl.loop(end, end + 2)
    def _(tick):
        service(tick)

    ec.wait_recv()
    eyparts[...] = eparts[...] + erecv_c[...]
    ey = remote(eyparts, erecv_y, ey_sem.at[0], ey_sem.at[1], over_y)
    ey.start()

    @pl.loop(end + 2, end + 6)
    def _(tick):
        service(tick)

    ey.wait_recv()
    ezparts[...] = eyparts[...] + erecv_y[...]
    ez = [
        remote(ezparts, erecv_z.at[k - 1], ez_send.at[k - 1], ez_recv.at[k - 1], over_z[k - 1])
        for k in range(1, planes)
    ]
    for copy in ez:
        copy.start()

    @pl.loop(end + 6, end + 10)
    def _(tick):
        service(tick)

    esum = ezparts[...]
    for k in range(1, planes):
        ez[k - 1].wait_recv()
        esum += erecv_z[k - 1]
    for w in range(walkers):
        energy_ref[w] = -0.5 * scale * jnp.sum(esum[w])
    for copy in [ec, ey] + ez:
        copy.wait_send()

    @pl.loop(0, walkers)
    def _(w):
        for k in range(1, planes):
            copy_gz(w, k).wait_send()
        for k in range(planes):
            copy_gy(w, k).wait_send()
        for k in range(COLUMNS):
            copy_gc(w, k).wait_send()

    @pl.loop(0, units)
    def _(u):
        copy_rc(u).wait_send()
        copy_ry(u).wait_send()
        for k in range(1, planes):
            copy_rz(u, k).wait_send()


def per_device_kernel(green, chol_vecs, cotangent):
    walkers, rows, basis = green.shape
    count, occupied, _ = chol_vecs.shape
    devices = lax.axis_size("chol")
    planes = devices // (CORES * COLUMNS)
    scale = 1.0 / (occupied * count * devices)
    per = max(i for i in (1, 2, 3) if count % i == 0)
    loads = count // per
    bf16, f32 = jnp.bfloat16, jnp.float32
    block = (rows, basis)
    chunk = 256 if basis % 256 == 0 else 128
    units = walkers * (basis // chunk)
    piece = (rows, chunk)
    dma = pltpu.SemaphoreType.DMA
    others = planes - 1
    estack = (walkers, 8, 128)
    energy, own_rows = pl.pallas_call(
        functools.partial(exchange_kernel, scale),
        out_shape=(
            jax.ShapeDtypeStruct((walkers,), f32),
            jax.ShapeDtypeStruct((walkers,) + block, f32),
        ),
        in_specs=[
            pl.BlockSpec(memory_space=pltpu.HBM),
            pl.BlockSpec(memory_space=pltpu.HBM),
        ],
        out_specs=(
            pl.BlockSpec(memory_space=pltpu.SMEM),
            pl.BlockSpec(memory_space=pltpu.VMEM),
        ),
        scratch_shapes=[
            pltpu.VMEM((count, occupied, basis), bf16),
            pltpu.VMEM((walkers, planes, COLUMNS, CORES) + block, bf16),
            pltpu.VMEM((occupied, count * occupied), bf16),
            pltpu.VMEM((units, CORES, COLUMNS, planes) + piece, f32),
            pltpu.VMEM((units, CORES, COLUMNS, planes) + piece, bf16),
            pltpu.VMEM((units, COLUMNS, planes) + piece, bf16),
            pltpu.VMEM((units, planes) + piece, bf16),
            pltpu.VMEM((units, planes) + piece, bf16),
            pltpu.VMEM((units, planes) + piece, f32),
            pltpu.VMEM((units, planes) + piece, bf16),
            pltpu.VMEM((units, others) + piece, bf16),
            pltpu.VMEM((units,) + piece, f32),
            pltpu.VMEM(estack, f32),
            pltpu.VMEM(estack, f32),
            pltpu.VMEM(estack, f32),
            pltpu.VMEM(estack, f32),
            pltpu.VMEM(estack, f32),
            pltpu.VMEM((others,) + estack, f32),
            dma((loads,)), dma((walkers,)),
            dma((walkers, others)), dma((walkers, others)),
            dma((walkers, planes)), dma((walkers, planes)),
            dma((walkers, COLUMNS)), dma((walkers, COLUMNS)),
            dma((units,)), dma((units,)),
            dma((units,)), dma((units,)),
            dma((units, others)), dma((units, others)),
            dma((2,)), dma((2,)),
            dma((others,)), dma((others,)),
        ],
        compiler_params=pltpu.CompilerParams(
            collective_id=0, has_side_effects=True, vmem_limit_bytes=48 * 1024 * 1024
        ),
        cost_estimate=pl.CostEstimate(
            flops=4 * walkers * count * occupied * occupied * basis,
            bytes_accessed=2 * chol_vecs.size,
            transcendentals=0,
        ),
    )(green, chol_vecs)
    grad_green = cotangent[:, None, None] * own_rows
    return (energy, grad_green)


def per_device_plain(green, chol_vecs, cotangent):
    count = chol_vecs.shape[0]
    walkers = green.shape[0]
    occupied = chol_vecs.shape[1]
    basis = chol_vecs.shape[2]
    scale = 1.0 / (occupied * count * lax.axis_size("chol"))
    full_green = lax.all_gather(green, "chol", axis=1, tiled=True)
    per_block = 4 if count % 4 == 0 else 1
    blocks = chol_vecs.reshape(count // per_block, per_block, occupied, basis)

    def step(carry, lblock):
        energy_acc, grad_acc = carry
        tmat = jnp.einsum("gip,wjp->wgij", lblock, full_green, preferred_element_type=jnp.float32)
        pairs = jnp.einsum("wgij,wgji->w", tmat, tmat)
        thalf = tmat.astype(jnp.bfloat16)
        gpart = jnp.einsum("wgki,gip->wkp", thalf, lblock, preferred_element_type=jnp.float32)
        return ((energy_acc + pairs, grad_acc + gpart), None)

    start = (jnp.zeros((walkers,), jnp.float32), jnp.zeros((walkers, occupied, basis), jnp.float32))
    (energy_part, grad_part), unused = lax.scan(step, start, blocks)
    energy_sum = lax.psum(energy_part, "chol")
    own_rows = lax.psum_scatter(grad_part, "chol", scatter_dimension=1, tiled=True)
    energy = -0.5 * scale * energy_sum
    grad_green = -scale * cotangent[:, None, None] * own_rows
    return (energy, grad_green)


def per_device(green, chol_vecs, cotangent):
    devices = lax.axis_size("chol")
    fits = (
        devices % (CORES * COLUMNS) == 0
        and devices > CORES * COLUMNS
        and green.shape[1] % 16 == 0
        and chol_vecs.shape[1] % 128 == 0
        and chol_vecs.shape[2] % 128 == 0
    )
    run = per_device_kernel if fits else per_device_plain
    return run(green, chol_vecs, cotangent)


def solution(mesh):
    placed = (P("groups", "chol", None), P("chol", None, None), P("groups"))
    return jax.shard_map(
        per_device,
        mesh=mesh,
        in_specs=placed,
        out_specs=(P("groups"), P("groups", "chol", None)),
        check_vma=False,
    )
```

```python
import functools

import jax
import jax.numpy as jnp
from jax import lax
from jax.experimental import pallas as pl
from jax.experimental.pallas import tpu as pltpu
from jax.sharding import PartitionSpec as P

CORES = 2
COLUMNS = 2


def exchange_kernel(
    scale,
    green_ref, chol_ref,
    energy_ref, grad_ref,
    vecs, full, half, partial, pair, ysend, yrecv, kept, zsend, zrecv, final,
    eparts, eyparts, ezparts, erecv_c, erecv_y, erecv_z,
    load_sem, own_sem, gu_send, gu_recv, gd_send, gd_recv, gy_send, gy_recv, gc_send, gc_recv,
    rc_send, rc_recv, ry_send, ry_recv, rz_send, rz_recv,
    ec_sem, ey_sem, ez_send, ez_recv,
):
    walkers, rows, basis = green_ref.shape
    count, occupied, _ = chol_ref.shape
    planes = full.shape[1]
    bf16, f32 = jnp.bfloat16, jnp.float32

    me = lax.axis_index("chol")
    c = lax.rem(me, CORES)
    y = lax.rem(me // CORES, COLUMNS)
    z = me // (CORES * COLUMNS)

    def device(zz, yy, cc):
        return {"chol": (zz * COLUMNS + yy) * CORES + cc}

    plane = [lax.rem(z + k, planes) for k in range(planes)]
    over_z = [device(plane[k], y, c) for k in range(1, planes)]
    over_y = device(z, 1 - y, c)
    over_c = device(z, y, 1 - c)

    own = [pltpu.make_async_copy(green_ref.at[w], full.at[w, z, y, c], own_sem.at[w]) for w in range(walkers)]
    for copy in own:
        copy.start()
    loads = load_sem.shape[0]
    per = count // loads

    def load(i):
        return pltpu.make_async_copy(
            chol_ref.at[pl.ds(i * per, per)], vecs.at[pl.ds(i * per, per)], load_sem.at[i]
        )

    for i in range(loads):
        load(i).start()

    barrier = pltpu.get_barrier_semaphore()
    for peer in over_z + [over_y, over_c]:
        pl.semaphore_signal(barrier, inc=1, device_id=peer, device_id_type=pl.DeviceIdType.MESH)
    pl.semaphore_wait(barrier, planes + 1)

    def remote(src, dst, send_sem, recv_sem, peer):
        return pltpu.make_async_remote_copy(
            src_ref=src, dst_ref=dst, send_sem=send_sem, recv_sem=recv_sem,
            device_id=peer, device_id_type=pl.DeviceIdType.MESH,
        )

    above = device(jnp.minimum(z + 1, planes - 1), y, c)
    below = device(jnp.maximum(z - 1, 0), y, c)

    def copy_up(w, h, s):
        block = full.at[w, s, y, c]
        return remote(block, block, gu_send.at[w, h - 1], gu_recv.at[w, h - 1], above)

    def copy_down(w, h, s):
        block = full.at[w, s, y, c]
        return remote(block, block, gd_send.at[w, h - 1], gd_recv.at[w, h - 1], below)

    def copy_gy(w, s):
        block = full.at[w, s, y, c]
        return remote(block, block, gy_send.at[w, s], gy_recv.at[w, s], over_y)

    def copy_gc(w, k):
        column = full.at[w, :, y if k == 0 else 1 - y, c]
        return remote(column, column, gc_send.at[w, k], gc_recv.at[w, k], over_c)

    def copy_rc(u):
        return remote(partial.at[u, 1 - c], pair.at[u], rc_send.at[u], rc_recv.at[u], over_c)

    def copy_ry(u):
        return remote(ysend.at[u], yrecv.at[u], ry_send.at[u], ry_recv.at[u], over_y)

    def copy_rz(u, k):
        return remote(
            zsend.at[u, plane[k]], zrecv.at[u, k - 1], rz_send.at[u, k - 1], rz_recv.at[u, k - 1], over_z[k - 1]
        )

    def offer(w):
        pltpu.make_async_copy(green_ref.at[w], full.at[w, z, y, c], own_sem.at[w]).wait()
        @pl.when(z + 1 < planes)
        def _():
            copy_up(w, 1, z).start()

        @pl.when(z > 0)
        def _():
            copy_down(w, 1, z).start()

        copy_gy(w, z).start()

    def gather_hop(w, h):
        @pl.when(z - h >= 0)
        def _():
            copy_up(w, h, z - h).wait_recv()

            @pl.when(z + 1 < planes)
            def _():
                copy_up(w, h + 1, z - h).start()

            copy_gy(w, z - h).start()

        @pl.when(z + h < planes)
        def _():
            copy_down(w, h, z + h).wait_recv()

            @pl.when(z > 0)
            def _():
                copy_down(w, h + 1, z + h).start()

            copy_gy(w, z + h).start()

    def gather_z(w, first=1):
        for h in range(first, planes):
            gather_hop(w, h)
        copy_gc(w, 0).start()

    def gather_y(w):
        for k in range(planes):
            copy_gy(w, k).wait_recv()
        copy_gc(w, 1).start()

    def gather_c(w):
        for k in range(COLUMNS):
            copy_gc(w, k).wait_recv()

    units, chunk = partial.shape[0], partial.shape[-1]
    chunks = basis // chunk
    period = loads + chunks

    def reduce_y(u):
        copy_rc(u).wait_recv()
        ysend[u] = (partial[u, c, 1 - y] + pair[u, 1 - y]).astype(bf16)
        copy_ry(u).start()
        kept[u] = partial[u, c, y] + pair[u, y]

    def reduce_z(u):
        copy_ry(u).wait_recv()
        zsend[u] = (kept[u] + yrecv[u].astype(f32)).astype(bf16)
        for k in range(planes - 1, 0, -1):
            copy_rz(u, k).start()
        final[u] = kept[u, z] + yrecv[u, z].astype(f32)

    def finish(u):
        total = final[u]
        for k in range(1, planes):
            copy_rz(u, k).wait_recv()
            total += zrecv[u, k - 1].astype(f32)
        at = pl.multiple_of(lax.rem(u, chunks) * chunk, chunk)
        grad_ref[u // chunks, :, pl.ds(at, chunk)] = -scale * total

    def service(tick):
        for lag, stage in ((2, reduce_y), (6, reduce_z), (10, finish)):
            made = tick - lag
            place = lax.rem(made + 2 * period, period) - loads
            unit = (made + 2 * period) // period * chunks - 2 * chunks + place

            @pl.when((place >= 0) & (unit >= 0) & (unit < units))
            def _():
                stage(unit)

    def make_tmat(w):
        @pl.loop(0, loads)
        def _(i):
            first = i * per
            left = vecs[pl.ds(first, per)].reshape(per * occupied, basis)
            right = full[w].reshape(occupied, basis)
            tmat = lax.dot_general(left, right, (((1,), (1,)), ((), ())), preferred_element_type=f32)
            for j in range(per):
                at = pl.multiple_of((first + j) * occupied, occupied)
                half[:, pl.ds(at, occupied)] = tmat[j * occupied:(j + 1) * occupied].astype(bf16)
            service(w * period + i)

            @pl.when((w + 2 < walkers) & (i + 1 < planes))
            def _():
                gather_hop(w + 2, i + 1)


    def make_grad(w):
        eparts[w] = jnp.zeros(eparts.shape[1:], f32)

        @pl.loop(0, chunks)
        def _(i):
            at = pl.multiple_of(i * chunk, chunk)
            right = vecs[:, :, pl.ds(at, chunk)].reshape(count * occupied, chunk)
            part = jnp.dot(half[...], right, preferred_element_type=f32)
            green = full[w, :, :, :, :, pl.ds(at, chunk)].reshape(occupied, chunk)
            folded = (part * green.astype(f32)).reshape(occupied // 8, 8, chunk).sum(axis=0)
            for lane in range(0, chunk, 128):
                eparts[w] += folded[:, lane:lane + 128]
            for zz in range(planes):
                for yy in range(COLUMNS):
                    for cc in range(CORES):
                        row = ((zz * COLUMNS + yy) * CORES + cc) * rows
                        partial[w * chunks + i, cc, yy, zz] = part[row:row + rows]
            copy_rc(w * chunks + i).start()
            service(w * period + loads + i)

    for w in range(walkers):
        offer(w)
    gather_z(0)
    gather_y(0)
    if walkers > 1:
        gather_z(1)
    gather_c(0)
    for i in range(loads):
        load(i).wait()

    @pl.loop(0, walkers)
    def _(w):
        make_tmat(w)

        @pl.when(w + 2 < walkers)
        def _():
            gather_z(w + 2, loads + 1)

        @pl.when(w + 1 < walkers)
        def _():
            gather_y(w + 1)

        make_grad(w)

        @pl.when(w + 1 < walkers)
        def _():
            gather_c(w + 1)

    end = walkers * period
    ec = remote(eparts, erecv_c, ec_sem.at[0], ec_sem.at[1], over_c)
    ec.start()

    @pl.loop(end, end + 2)
    def _(tick):
        service(tick)

    ec.wait_recv()
    eyparts[...] = eparts[...] + erecv_c[...]
    ey = remote(eyparts, erecv_y, ey_sem.at[0], ey_sem.at[1], over_y)
    ey.start()

    @pl.loop(end + 2, end + 6)
    def _(tick):
        service(tick)

    ey.wait_recv()
    ezparts[...] = eyparts[...] + erecv_y[...]
    ez = [
        remote(ezparts, erecv_z.at[k - 1], ez_send.at[k - 1], ez_recv.at[k - 1], over_z[k - 1])
        for k in range(1, planes)
    ]
    for copy in ez:
        copy.start()

    @pl.loop(end + 6, end + 10)
    def _(tick):
        service(tick)

    esum = ezparts[...]
    for k in range(1, planes):
        ez[k - 1].wait_recv()
        esum += erecv_z[k - 1]
    for w in range(walkers):
        energy_ref[w] = -0.5 * scale * jnp.sum(esum[w])
    for copy in [ec, ey] + ez:
        copy.wait_send()

    @pl.loop(0, walkers)
    def _(w):
        for h in range(1, planes):
            @pl.when((z - (h - 1) >= 0) & (z + 1 < planes))
            def _():
                copy_up(w, h, z - (h - 1)).wait_send()

            @pl.when((z + (h - 1) < planes) & (z > 0))
            def _():
                copy_down(w, h, z + (h - 1)).wait_send()

        for k in range(planes):
            copy_gy(w, k).wait_send()
        for k in range(COLUMNS):
            copy_gc(w, k).wait_send()

    @pl.loop(0, units)
    def _(u):
        copy_rc(u).wait_send()
        copy_ry(u).wait_send()
        for k in range(1, planes):
            copy_rz(u, k).wait_send()


def per_device_kernel(green, chol_vecs, cotangent):
    walkers, rows, basis = green.shape
    count, occupied, _ = chol_vecs.shape
    devices = lax.axis_size("chol")
    planes = devices // (CORES * COLUMNS)
    scale = 1.0 / (occupied * count * devices)
    per = max(i for i in (1, 2, 3) if count % i == 0)
    loads = count // per
    bf16, f32 = jnp.bfloat16, jnp.float32
    block = (rows, basis)
    chunk = 256 if basis % 256 == 0 else 128
    units = walkers * (basis // chunk)
    piece = (rows, chunk)
    dma = pltpu.SemaphoreType.DMA
    others = planes - 1
    estack = (walkers, 8, 128)
    energy, own_rows = pl.pallas_call(
        functools.partial(exchange_kernel, scale),
        out_shape=(
            jax.ShapeDtypeStruct((walkers,), f32),
            jax.ShapeDtypeStruct((walkers,) + block, f32),
        ),
        in_specs=[
            pl.BlockSpec(memory_space=pltpu.HBM),
            pl.BlockSpec(memory_space=pltpu.HBM),
        ],
        out_specs=(
            pl.BlockSpec(memory_space=pltpu.SMEM),
            pl.BlockSpec(memory_space=pltpu.VMEM),
        ),
        scratch_shapes=[
            pltpu.VMEM((count, occupied, basis), bf16),
            pltpu.VMEM((walkers, planes, COLUMNS, CORES) + block, bf16),
            pltpu.VMEM((occupied, count * occupied), bf16),
            pltpu.VMEM((units, CORES, COLUMNS, planes) + piece, f32),
            pltpu.VMEM((units, COLUMNS, planes) + piece, f32),
            pltpu.VMEM((units, planes) + piece, bf16),
            pltpu.VMEM((units, planes) + piece, bf16),
            pltpu.VMEM((units, planes) + piece, f32),
            pltpu.VMEM((units, planes) + piece, bf16),
            pltpu.VMEM((units, others) + piece, bf16),
            pltpu.VMEM((units,) + piece, f32),
            pltpu.VMEM(estack, f32),
            pltpu.VMEM(estack, f32),
            pltpu.VMEM(estack, f32),
            pltpu.VMEM(estack, f32),
            pltpu.VMEM(estack, f32),
            pltpu.VMEM((others,) + estack, f32),
            dma((loads,)), dma((walkers,)),
            dma((walkers, planes)), dma((walkers, planes)),
            dma((walkers, planes)), dma((walkers, planes)),
            dma((walkers, planes)), dma((walkers, planes)),
            dma((walkers, COLUMNS)), dma((walkers, COLUMNS)),
            dma((units,)), dma((units,)),
            dma((units,)), dma((units,)),
            dma((units, others)), dma((units, others)),
            dma((2,)), dma((2,)),
            dma((others,)), dma((others,)),
        ],
        compiler_params=pltpu.CompilerParams(
            collective_id=0, has_side_effects=True, vmem_limit_bytes=48 * 1024 * 1024
        ),
        cost_estimate=pl.CostEstimate(
            flops=4 * walkers * count * occupied * occupied * basis,
            bytes_accessed=2 * chol_vecs.size,
            transcendentals=0,
        ),
    )(green, chol_vecs)
    grad_green = cotangent[:, None, None] * own_rows
    return (energy, grad_green)


def per_device_plain(green, chol_vecs, cotangent):
    count = chol_vecs.shape[0]
    walkers = green.shape[0]
    occupied = chol_vecs.shape[1]
    basis = chol_vecs.shape[2]
    scale = 1.0 / (occupied * count * lax.axis_size("chol"))
    full_green = lax.all_gather(green, "chol", axis=1, tiled=True)
    per_block = 4 if count % 4 == 0 else 1
    blocks = chol_vecs.reshape(count // per_block, per_block, occupied, basis)

    def step(carry, lblock):
        energy_acc, grad_acc = carry
        tmat = jnp.einsum("gip,wjp->wgij", lblock, full_green, preferred_element_type=jnp.float32)
        pairs = jnp.einsum("wgij,wgji->w", tmat, tmat)
        thalf = tmat.astype(jnp.bfloat16)
        gpart = jnp.einsum("wgki,gip->wkp", thalf, lblock, preferred_element_type=jnp.float32)
        return ((energy_acc + pairs, grad_acc + gpart), None)

    start = (jnp.zeros((walkers,), jnp.float32), jnp.zeros((walkers, occupied, basis), jnp.float32))
    (energy_part, grad_part), unused = lax.scan(step, start, blocks)
    energy_sum = lax.psum(energy_part, "chol")
    own_rows = lax.psum_scatter(grad_part, "chol", scatter_dimension=1, tiled=True)
    energy = -0.5 * scale * energy_sum
    grad_green = -scale * cotangent[:, None, None] * own_rows
    return (energy, grad_green)


def per_device(green, chol_vecs, cotangent):
    devices = lax.axis_size("chol")
    fits = (
        devices % (CORES * COLUMNS) == 0
        and devices > CORES * COLUMNS
        and green.shape[1] % 16 == 0
        and chol_vecs.shape[1] % 128 == 0
        and chol_vecs.shape[2] % 128 == 0
    )
    run = per_device_kernel if fits else per_device_plain
    return run(green, chol_vecs, cotangent)


def solution(mesh):
    placed = (P("groups", "chol", None), P("chol", None, None), P("groups"))
    return jax.shard_map(
        per_device,
        mesh=mesh,
        in_specs=placed,
        out_specs=(P("groups"), P("groups", "chol", None)),
        check_vma=False,
    )
```

```python
import functools

import jax
import jax.numpy as jnp
from jax import lax
from jax.experimental import pallas as pl
from jax.experimental.pallas import tpu as pltpu
from jax.sharding import PartitionSpec as P

CORES = 2
COLUMNS = 2


def exchange_kernel(
    scale,
    green_ref, chol_ref,
    energy_ref, grad_ref,
    vecs, full, half, partial, pair, ysend, yrecv, kept, zsend, zrecv, final,
    eparts, eyparts, ezparts, erecv_c, erecv_y, erecv_z,
    load_sem, own_sem, gz_send, gz_recv, gy_send, gy_recv, gc_send, gc_recv,
    rc_send, rc_recv, ry_send, ry_recv, rz_send, rz_recv,
    ec_sem, ey_sem, ez_send, ez_recv,
):
    walkers, rows, basis = green_ref.shape
    count, occupied, _ = chol_ref.shape
    planes = full.shape[1]
    bf16, f32 = jnp.bfloat16, jnp.float32

    me = lax.axis_index("chol")
    c = lax.rem(me, CORES)
    y = lax.rem(me // CORES, COLUMNS)
    z = me // (CORES * COLUMNS)

    def device(zz, yy, cc):
        return {"chol": (zz * COLUMNS + yy) * CORES + cc}

    plane = [lax.rem(z + k, planes) for k in range(planes)]
    source = [lax.rem(z - k + planes, planes) for k in range(planes)]
    over_z = [device(plane[k], y, c) for k in range(1, planes)]
    over_y = device(z, 1 - y, c)
    across = [device(plane[k], 1 - y, c) for k in range(1, planes)]
    over_c = device(z, y, 1 - c)

    own = [pltpu.make_async_copy(green_ref.at[w], full.at[w, z, y, c], own_sem.at[w]) for w in range(walkers)]
    for copy in own:
        copy.start()
    loads = load_sem.shape[0]
    per = count // loads

    def load(i):
        return pltpu.make_async_copy(
            chol_ref.at[pl.ds(i * per, per)], vecs.at[pl.ds(i * per, per)], load_sem.at[i]
        )

    for i in range(loads):
        load(i).start()

    barrier = pltpu.get_barrier_semaphore()
    for peer in over_z + across + [over_y, over_c]:
        pl.semaphore_signal(barrier, inc=1, device_id=peer, device_id_type=pl.DeviceIdType.MESH)
    pl.semaphore_wait(barrier, 2 * planes)

    def remote(src, dst, send_sem, recv_sem, peer):
        return pltpu.make_async_remote_copy(
            src_ref=src, dst_ref=dst, send_sem=send_sem, recv_sem=recv_sem,
            device_id=peer, device_id_type=pl.DeviceIdType.MESH,
        )

    def copy_gz(w, k):
        block = full.at[w, z, y, c]
        return remote(block, block, gz_send.at[w, k - 1], gz_recv.at[w, k - 1], over_z[k - 1])

    def copy_gy(w, k):
        block = full.at[w, source[k], y, c]
        return remote(block, block, gy_send.at[w, k], gy_recv.at[w, k], over_y)

    def copy_gc(w, k):
        column = full.at[w, :, y if k == 0 else 1 - y, c]
        return remote(column, column, gc_send.at[w, k], gc_recv.at[w, k], over_c)

    def copy_rc(u):
        return remote(partial.at[u, 1 - c], pair.at[u], rc_send.at[u], rc_recv.at[u], over_c)

    def copy_ry(u):
        return remote(ysend.at[u], yrecv.at[u], ry_send.at[u], ry_recv.at[u], over_y)

    def copy_rz(u, k):
        return remote(
            zsend.at[u, plane[k]], zrecv.at[u, k - 1], rz_send.at[u, k - 1], rz_recv.at[u, k - 1], over_z[k - 1]
        )

    def offer(w):
        pltpu.make_async_copy(green_ref.at[w], full.at[w, z, y, c], own_sem.at[w]).wait()
        for k in range(planes - 1, 0, -1):
            copy_gz(w, k).start()
        copy_gy(w, 0).start()
        if w == 0:
            block = full.at[w, z, y, c]
            for k in range(planes - 1, 0, -1):
                remote(block, block, gy_send.at[w, k], gy_recv.at[w, k], across[k - 1]).start()

    def gather_z(w):
        for k in range(1, planes):
            copy_gz(w, k).wait_recv()
            if type(w) is not int or w > 0:
                copy_gy(w, k).start()
        copy_gc(w, 0).start()

    def gather_y(w):
        for k in range(planes):
            copy_gy(w, k).wait_recv()
        copy_gc(w, 1).start()

    def gather_c(w):
        for k in range(COLUMNS):
            copy_gc(w, k).wait_recv()

    units, chunk = partial.shape[0], partial.shape[-1]
    chunks = basis // chunk
    period = loads + chunks

    def reduce_y(u):
        copy_rc(u).wait_recv()
        ysend[u] = (partial[u, c, 1 - y] + pair[u, 1 - y]).astype(bf16)
        copy_ry(u).start()
        kept[u] = partial[u, c, y] + pair[u, y]

    def reduce_z(u):
        copy_ry(u).wait_recv()
        zsend[u] = (kept[u] + yrecv[u].astype(f32)).astype(bf16)
        for k in range(planes - 1, 0, -1):
            copy_rz(u, k).start()
        final[u] = kept[u, z] + yrecv[u, z].astype(f32)

    def finish(u):
        total = final[u]
        for k in range(1, planes):
            copy_rz(u, k).wait_recv()
            total += zrecv[u, k - 1].astype(f32)
        at = pl.multiple_of(lax.rem(u, chunks) * chunk, chunk)
        grad_ref[u // chunks, :, pl.ds(at, chunk)] = -scale * total

    def service(tick):
        for lag, stage in ((2, reduce_y), (6, reduce_z), (10, finish)):
            made = tick - lag
            place = lax.rem(made + 2 * period, period) - loads
            unit = (made + 2 * period) // period * chunks - 2 * chunks + place

            @pl.when((place >= 0) & (unit >= 0) & (unit < units))
            def _():
                stage(unit)

    def make_tmat(w):
        @pl.loop(0, loads)
        def _(i):
            first = i * per
            left = vecs[pl.ds(first, per)].reshape(per * occupied, basis)
            right = full[w].reshape(occupied, basis)
            tmat = lax.dot_general(left, right, (((1,), (1,)), ((), ())), preferred_element_type=f32)
            for j in range(per):
                at = pl.multiple_of((first + j) * occupied, occupied)
                half[:, pl.ds(at, occupied)] = tmat[j * occupied:(j + 1) * occupied].astype(bf16)
            service(w * period + i)

    def make_grad(w):
        eparts[w] = jnp.zeros(eparts.shape[1:], f32)

        @pl.loop(0, chunks)
        def _(i):
            at = pl.multiple_of(i * chunk, chunk)
            right = vecs[:, :, pl.ds(at, chunk)].reshape(count * occupied, chunk)
            part = jnp.dot(half[...], right, preferred_element_type=f32)
            green = full[w, :, :, :, :, pl.ds(at, chunk)].reshape(occupied, chunk)
            folded = (part * green.astype(f32)).reshape(occupied // 8, 8, chunk).sum(axis=0)
            for lane in range(0, chunk, 128):
                eparts[w] += folded[:, lane:lane + 128]
            for zz in range(planes):
                for yy in range(COLUMNS):
                    for cc in range(CORES):
                        row = ((zz * COLUMNS + yy) * CORES + cc) * rows
                        partial[w * chunks + i, cc, yy, zz] = part[row:row + rows]
            copy_rc(w * chunks + i).start()
            service(w * period + loads + i)

    for w in range(walkers):
        offer(w)
    gather_z(0)
    gather_y(0)
    if walkers > 1:
        gather_z(1)
    gather_c(0)
    for i in range(loads):
        load(i).wait()

    @pl.loop(0, walkers)
    def _(w):
        make_tmat(w)

        @pl.when(w + 2 < walkers)
        def _():
            gather_z(w + 2)

        @pl.when(w + 1 < walkers)
        def _():
            gather_y(w + 1)

        make_grad(w)

        @pl.when(w + 1 < walkers)
        def _():
            gather_c(w + 1)

    end = walkers * period
    ec = remote(eparts, erecv_c, ec_sem.at[0], ec_sem.at[1], over_c)
    ec.start()

    @pl.loop(end, end + 2)
    def _(tick):
        service(tick)

    ec.wait_recv()
    eyparts[...] = eparts[...] + erecv_c[...]
    ey = remote(eyparts, erecv_y, ey_sem.at[0], ey_sem.at[1], over_y)
    ey.start()

    @pl.loop(end + 2, end + 6)
    def _(tick):
        service(tick)

    ey.wait_recv()
    ezparts[...] = eyparts[...] + erecv_y[...]
    ez = [
        remote(ezparts, erecv_z.at[k - 1], ez_send.at[k - 1], ez_recv.at[k - 1], over_z[k - 1])
        for k in range(1, planes)
    ]
    for copy in ez:
        copy.start()

    @pl.loop(end + 6, end + 10)
    def _(tick):
        service(tick)

    esum = ezparts[...]
    for k in range(1, planes):
        ez[k - 1].wait_recv()
        esum += erecv_z[k - 1]
    for w in range(walkers):
        energy_ref[w] = -0.5 * scale * jnp.sum(esum[w])
    for copy in [ec, ey] + ez:
        copy.wait_send()

    @pl.loop(0, walkers)
    def _(w):
        for k in range(1, planes):
            copy_gz(w, k).wait_send()
        for k in range(planes):
            copy_gy(w, k).wait_send()
        for k in range(COLUMNS):
            copy_gc(w, k).wait_send()

    @pl.loop(0, units)
    def _(u):
        copy_rc(u).wait_send()
        copy_ry(u).wait_send()
        for k in range(1, planes):
            copy_rz(u, k).wait_send()


def per_device_kernel(green, chol_vecs, cotangent):
    walkers, rows, basis = green.shape
    count, occupied, _ = chol_vecs.shape
    devices = lax.axis_size("chol")
    planes = devices // (CORES * COLUMNS)
    scale = 1.0 / (occupied * count * devices)
    per = max(i for i in (1, 2, 3) if count % i == 0)
    loads = count // per
    bf16, f32 = jnp.bfloat16, jnp.float32
    block = (rows, basis)
    chunk = 256 if basis % 256 == 0 else 128
    units = walkers * (basis // chunk)
    piece = (rows, chunk)
    dma = pltpu.SemaphoreType.DMA
    others = planes - 1
    estack = (walkers, 8, 128)
    energy, own_rows = pl.pallas_call(
        functools.partial(exchange_kernel, scale),
        out_shape=(
            jax.ShapeDtypeStruct((walkers,), f32),
            jax.ShapeDtypeStruct((walkers,) + block, f32),
        ),
        in_specs=[
            pl.BlockSpec(memory_space=pltpu.HBM),
            pl.BlockSpec(memory_space=pltpu.HBM),
        ],
        out_specs=(
            pl.BlockSpec(memory_space=pltpu.SMEM),
            pl.BlockSpec(memory_space=pltpu.VMEM),
        ),
        scratch_shapes=[
            pltpu.VMEM((count, occupied, basis), bf16),
            pltpu.VMEM((walkers, planes, COLUMNS, CORES) + block, bf16),
            pltpu.VMEM((occupied, count * occupied), bf16),
            pltpu.VMEM((units, CORES, COLUMNS, planes) + piece, f32),
            pltpu.VMEM((units, COLUMNS, planes) + piece, f32),
            pltpu.VMEM((units, planes) + piece, bf16),
            pltpu.VMEM((units, planes) + piece, bf16),
            pltpu.VMEM((units, planes) + piece, f32),
            pltpu.VMEM((units, planes) + piece, bf16),
            pltpu.VMEM((units, others) + piece, bf16),
            pltpu.VMEM((units,) + piece, f32),
            pltpu.VMEM(estack, f32),
            pltpu.VMEM(estack, f32),
            pltpu.VMEM(estack, f32),
            pltpu.VMEM(estack, f32),
            pltpu.VMEM(estack, f32),
            pltpu.VMEM((others,) + estack, f32),
            dma((loads,)), dma((walkers,)),
            dma((walkers, others)), dma((walkers, others)),
            dma((walkers, planes)), dma((walkers, planes)),
            dma((walkers, COLUMNS)), dma((walkers, COLUMNS)),
            dma((units,)), dma((units,)),
            dma((units,)), dma((units,)),
            dma((units, others)), dma((units, others)),
            dma((2,)), dma((2,)),
            dma((others,)), dma((others,)),
        ],
        compiler_params=pltpu.CompilerParams(
            collective_id=0, has_side_effects=True, vmem_limit_bytes=48 * 1024 * 1024
        ),
        cost_estimate=pl.CostEstimate(
            flops=4 * walkers * count * occupied * occupied * basis,
            bytes_accessed=2 * chol_vecs.size,
            transcendentals=0,
        ),
    )(green, chol_vecs)
    grad_green = cotangent[:, None, None] * own_rows
    return (energy, grad_green)


def per_device_plain(green, chol_vecs, cotangent):
    count = chol_vecs.shape[0]
    walkers = green.shape[0]
    occupied = chol_vecs.shape[1]
    basis = chol_vecs.shape[2]
    scale = 1.0 / (occupied * count * lax.axis_size("chol"))
    full_green = lax.all_gather(green, "chol", axis=1, tiled=True)
    per_block = 4 if count % 4 == 0 else 1
    blocks = chol_vecs.reshape(count // per_block, per_block, occupied, basis)

    def step(carry, lblock):
        energy_acc, grad_acc = carry
        tmat = jnp.einsum("gip,wjp->wgij", lblock, full_green, preferred_element_type=jnp.float32)
        pairs = jnp.einsum("wgij,wgji->w", tmat, tmat)
        thalf = tmat.astype(jnp.bfloat16)
        gpart = jnp.einsum("wgki,gip->wkp", thalf, lblock, preferred_element_type=jnp.float32)
        return ((energy_acc + pairs, grad_acc + gpart), None)

    start = (jnp.zeros((walkers,), jnp.float32), jnp.zeros((walkers, occupied, basis), jnp.float32))
    (energy_part, grad_part), unused = lax.scan(step, start, blocks)
    energy_sum = lax.psum(energy_part, "chol")
    own_rows = lax.psum_scatter(grad_part, "chol", scatter_dimension=1, tiled=True)
    energy = -0.5 * scale * energy_sum
    grad_green = -scale * cotangent[:, None, None] * own_rows
    return (energy, grad_green)


def per_device(green, chol_vecs, cotangent):
    devices = lax.axis_size("chol")
    fits = (
        devices % (CORES * COLUMNS) == 0
        and devices > CORES * COLUMNS
        and green.shape[1] % 16 == 0
        and chol_vecs.shape[1] % 128 == 0
        and chol_vecs.shape[2] % 128 == 0
    )
    run = per_device_kernel if fits else per_device_plain
    return run(green, chol_vecs, cotangent)


def solution(mesh):
    placed = (P("groups", "chol", None), P("chol", None, None), P("groups"))
    return jax.shard_map(
        per_device,
        mesh=mesh,
        in_specs=placed,
        out_specs=(P("groups"), P("groups", "chol", None)),
        check_vma=False,
    )
```
